1024 devices in a mesh: outer: 64 (over x, z), inner: 16 (over y, core).
Axes of the slice: x: 4, y: 8, z: 16, core: 2. Of those that a mesh axis runs over, the one named last changes fastest.
Arguments:
- hidden_in: bfloat16 [131072, 896], P(('outer', 'inner')), may hold values from -6 to 6
- doc_ids: int32 [1024, 128], P(('outer', 'inner')), may hold values from 0 to 7, never falling along the last dimension, each value on 1 to 32 neighbouring positions
- grad_mixed: bfloat16 [131072, 896], P(('outer', 'inner')), may hold values from -6 to 6
- in_codes: bfloat16 [896, 576], P('inner'), may hold values from -1.8708287 to 1.8708287
- in_scales: float32 [28, 9], replicated, may hold values from 0.5 to 2
- out_codes: bfloat16 [448, 896], P(None, 'inner'), may hold values from -0.25 to 0.25
- out_scales: float32 [7, 28], replicated, may hold values from 0.5 to 2
Outputs:
- mixed: bfloat16 [131072, 896], P(('outer', 'inner'))
- grad_hidden: bfloat16 [131072, 896], P(('outer', 'inner'))
- grad_in_weight: float32 [516096], P(('outer', 'inner'))
- grad_out_weight: float32 [401408], P(('outer', 'inner'))
The draws below stay inside these ranges and needn't reach their ends.
All inputs are finite; a program needn't handle non-finite values.
Results may differ from the reference program's by a relative error of at most 0.015.
Values may be sent and summed in bfloat16 or wider, within the bound.
A program may use at most 32 MiB of HBM per device.

```python
import math
import jax
import jax.numpy as jnp
import numpy as np
from jax import lax

D = 896
HEAD_SIZE = 64
QUERY_HEADS = 7
KEY_VALUE_HEADS = 1
SB = 32
DOCS = 8
TOK_DEV = 128
QUERY_COLUMNS = 448
KEY_COLUMNS = 64
QKV_W = 576
TOKENS = 131072
DEVICES = 1024


def draw_in_codes(key, part):
    key = jax.random.fold_in(key, 11)
    values = jnp.clip(jax.random.normal(key, (D, QKV_W), jnp.float32), -6.0, 6.0)
    return (values * D ** (-0.5)).astype(jnp.bfloat16)


def level_of(key, dims, cuts, smallest, largest):
    loudness = 1.0
    for dim, blocks in cuts:
        steps = jax.random.uniform(jax.random.fold_in(jax.random.fold_in(key, 6), dim), (blocks,), jnp.float32, smallest / len(cuts), largest / len(cuts))
        loudness = loudness * jnp.repeat(jnp.exp(steps), dims[dim] // blocks).reshape((-1,) + (1,) * (len(dims) - 1 - dim))
    return loudness


def profile(number_of, total, limit, slope):
    portions = [(1 << 20) // math.isqrt(grade ** slope) + 1 for grade in range(2, number_of + 1)]
    spare, holding = total - limit - (number_of - 1), [1] * (number_of - 1)
    while spare > 0:
        candidates = [i for i in range(number_of - 1) if holding[i] < limit]
        pool, remaining = sum([portions[i] for i in candidates]), spare
        for i in candidates:
            more = min(limit - holding[i], max(1, remaining * portions[i] // pool), spare)
            holding[i] = holding[i] + more
            spare = spare - more
    return np.array([limit] + holding)


def uneven_parts(key, count, total, most, slope):
    if count == 2:
        one = jax.random.randint(key, (), max(1, total - most), min(most, total - 1) + 1)
        return jnp.stack([one, total - one])
    tallies = jnp.asarray(profile(count, total, most, slope), jnp.int32)
    pairs = (count - 1) // 2
    giver, taker = tallies[1:1 + 2 * pairs:2], tallies[2:2 + 2 * pairs:2]
    margin = jnp.minimum(giver - 1, most - taker)
    passed = jax.random.randint(jax.random.fold_in(key, 1), (pairs,), 0, 1 << 20) % (margin + 1)
    tallies = tallies.at[1:1 + 2 * pairs:2].set(giver - passed).at[2:2 + 2 * pairs:2].set(taker + passed)
    return tallies[jax.random.permutation(jax.random.fold_in(key, 2), count)]


def normal_values(key, dims, spread, reach, pieces=(), held_as=jnp.bfloat16):
    gain = level_of(key, dims, pieces, -0.22, 0.18) if pieces else 1.0
    values = jax.random.normal(key, dims, jnp.float32) * spread * gain
    return jnp.minimum(jnp.maximum(values, -reach), reach).astype(held_as)


def setup_inputs(seed: int = 0) -> dict:
    arg_keys = jax.random.split(jax.random.key(seed), 8)
    return {
        "hidden_in": normal_values(arg_keys[0], (TOKENS, D), 1.0, 6.0, ((0, 1024),)),
        "doc_ids": jax.vmap(lambda own: jnp.searchsorted(jnp.cumsum(uneven_parts(own, DOCS, TOK_DEV, TOK_DEV // 4, 1)), jnp.arange(TOK_DEV), side="right"))(jax.random.split(arg_keys[1], DEVICES)).reshape((DEVICES, TOK_DEV)).astype(jnp.int32),
        "grad_mixed": normal_values(arg_keys[2], (TOKENS, D), 1.0, 6.0, ((0, 1024),)),
        "in_codes": draw_in_codes(jax.random.fold_in(arg_keys[7], 71), 0),
        "in_scales": jnp.clip(jnp.exp(jax.random.uniform(arg_keys[4], (D // SB, QKV_W // HEAD_SIZE), jnp.float32, math.log(0.5), math.log(2.0))), 0.5, 2.0),
        "out_codes": normal_values(arg_keys[5], (QUERY_COLUMNS, D), QUERY_COLUMNS ** -0.5, 0.25, ((1, 16),)),
        "out_scales": jnp.clip(jnp.exp(jax.random.uniform(arg_keys[6], (QUERY_COLUMNS // HEAD_SIZE, D // SB), jnp.float32, math.log(0.5), math.log(2.0))), 0.5, 2.0),
    }


rope_base = 1000000.0
norm_eps = 1e-06

def expand_scales(scales, row_block, col_block):
    return jnp.repeat(jnp.repeat(scales, row_block, axis=0), col_block, axis=1)

def dequantize(codes, scales, row_block, col_block):
    return (codes.astype(jnp.float32) * expand_scales(scales, row_block, col_block)).astype(jnp.bfloat16)

def rope_tables(row_docs):
    sequence_length = row_docs.shape[0]
    token_index = jnp.arange(sequence_length, dtype=jnp.int32)
    starting = jnp.concatenate([jnp.ones((1,), jnp.bool_), row_docs[1:] != row_docs[:-1]])
    doc_first = lax.cummax(jnp.where(starting, token_index, 0), axis=0)
    positions = (token_index - doc_first).astype(jnp.float32)
    half_width = HEAD_SIZE // 2
    frequency = rope_base ** (-jnp.arange(half_width, dtype=jnp.float32) * 2.0 / HEAD_SIZE)
    angles = positions[:, None] * frequency[None, :]
    return (jnp.cos(angles), jnp.sin(angles))

def apply_rotary(vectors, cosine_table, sines_lookup, direction):
    half_width = HEAD_SIZE // 2
    first_half = vectors[..., :half_width]
    second_half = vectors[..., half_width:]
    cos_b = cosine_table[:, None, :]
    sin_b = sines_lookup[:, None, :]
    return jnp.concatenate([first_half * cos_b - direction * second_half * sin_b, second_half * cos_b + direction * first_half * sin_b], axis=-1)

def normalize(rows_in):
    rows_f = rows_in.astype(jnp.float32)
    inverse_rms = lax.rsqrt(lax.optimization_barrier(jnp.mean(rows_f * rows_f, axis=-1, keepdims=True)) + norm_eps)
    return (rows_f * inverse_rms, inverse_rms)

def attend(projected_rows, row_docs):
    sequence_length = projected_rows.shape[0]
    query_group = QUERY_HEADS // KEY_VALUE_HEADS
    cosine_table, sines_lookup = rope_tables(row_docs)
    query_rows = apply_rotary(projected_rows[:, :QUERY_COLUMNS].reshape(sequence_length, QUERY_HEADS, HEAD_SIZE), cosine_table, sines_lookup, 1.0)
    query_rows_batch = query_rows.astype(jnp.bfloat16).reshape(sequence_length, KEY_VALUE_HEADS, query_group, HEAD_SIZE)
    key_rows_batch = apply_rotary(projected_rows[:, QUERY_COLUMNS:QUERY_COLUMNS + KEY_COLUMNS].reshape(sequence_length, KEY_VALUE_HEADS, HEAD_SIZE), cosine_table, sines_lookup, 1.0).astype(jnp.bfloat16)
    value_rows_batch = projected_rows[:, QUERY_COLUMNS + KEY_COLUMNS:].reshape(sequence_length, KEY_VALUE_HEADS, HEAD_SIZE).astype(jnp.bfloat16)
    scores = jnp.einsum('tkgd,skd->kgts', query_rows_batch.astype(jnp.float32), key_rows_batch.astype(jnp.float32)) * HEAD_SIZE ** (-0.5)
    token_index = jnp.arange(sequence_length, dtype=jnp.int32)
    allowed = (row_docs[:, None] == row_docs[None, :]) & (token_index[None, :] <= token_index[:, None])
    scores = jnp.where(allowed[None, None], scores, -jnp.inf)
    peak = lax.optimization_barrier(jnp.max(scores, axis=-1, keepdims=True))
    expon = jnp.exp(scores - peak)
    probs = expon / lax.optimization_barrier(jnp.sum(expon, axis=-1, keepdims=True))
    probs_b = probs.astype(jnp.bfloat16)
    attention_output = jnp.einsum('kgts,skd->tkgd', probs_b.astype(jnp.float32), value_rows_batch.astype(jnp.float32))
    attention_output = attention_output.reshape(sequence_length, QUERY_COLUMNS).astype(jnp.bfloat16)
    return (attention_output, (query_rows_batch, key_rows_batch, value_rows_batch, probs, probs_b, cosine_table, sines_lookup))

def attend_back(attention_output_gradient, attention_output, saved):
    query_rows_batch, key_rows_batch, value_rows_batch, probs, probs_b, cosine_table, sines_lookup = saved
    sequence_length = attention_output.shape[0]
    query_group = QUERY_HEADS // KEY_VALUE_HEADS
    head_gradients = attention_output_gradient.reshape(sequence_length, KEY_VALUE_HEADS, query_group, HEAD_SIZE).astype(jnp.float32)
    attention_heads = attention_output.reshape(sequence_length, KEY_VALUE_HEADS, query_group, HEAD_SIZE).astype(jnp.float32)
    grad_probs = jnp.einsum('tkgd,skd->kgts', head_gradients, value_rows_batch.astype(jnp.float32))
    delta = jnp.einsum('tkgd,tkgd->kgt', head_gradients, attention_heads)
    grad_scores = (probs * (grad_probs - delta[..., None]) * HEAD_SIZE ** (-0.5)).astype(jnp.bfloat16).astype(jnp.float32)
    grad_query = jnp.einsum('kgts,skd->tkgd', grad_scores, key_rows_batch.astype(jnp.float32))
    grad_keys = jnp.einsum('kgts,tkgd->skd', grad_scores, query_rows_batch.astype(jnp.float32))
    grad_values = jnp.einsum('kgts,tkgd->skd', probs_b.astype(jnp.float32), head_gradients)
    grad_query = apply_rotary(grad_query.reshape(sequence_length, QUERY_HEADS, HEAD_SIZE), cosine_table, sines_lookup, -1.0).reshape(sequence_length, QUERY_COLUMNS)
    grad_keys = apply_rotary(grad_keys, cosine_table, sines_lookup, -1.0).reshape(sequence_length, KEY_COLUMNS)
    joined = jnp.concatenate([grad_query, grad_keys, grad_values.reshape(sequence_length, KEY_COLUMNS)], axis=1)
    return joined.astype(jnp.bfloat16)

def reference(hidden_in, doc_ids, grad_mixed, in_codes, in_scales, out_codes, out_scales):
    w_in = dequantize(in_codes, in_scales, SB, HEAD_SIZE)
    w_out = dequantize(out_codes, out_scales, HEAD_SIZE, SB)
    grad_scale = TOKENS ** (-0.5)
    hidden_rows = hidden_in.reshape(DEVICES, TOK_DEV, D)
    grad_rows = grad_mixed.reshape(DEVICES, TOK_DEV, D)

    def one_device(carry, inputs):
        rows_x, row_docs, rows_grad = inputs
        normed, inverse_rms = normalize(rows_x)
        normed_b = normed.astype(jnp.bfloat16)
        projected_rows = jnp.dot(normed_b, w_in, preferred_element_type=jnp.float32)
        attention_output, saved = attend(projected_rows, row_docs)
        mixed_rows = (rows_x.astype(jnp.float32) + jnp.dot(attention_output, w_out, preferred_element_type=jnp.float32)).astype(jnp.bfloat16)
        attention_output_gradient = jnp.dot(rows_grad, w_out.T, preferred_element_type=jnp.float32).astype(jnp.bfloat16)
        grad_projected = attend_back(attention_output_gradient, attention_output, saved)
        grad_normed = jnp.dot(grad_projected, w_in.T, preferred_element_type=jnp.float32)
        inner_mean = lax.optimization_barrier(jnp.mean(grad_normed * normed, axis=-1, keepdims=True))
        grad_rows_in = ((grad_normed - normed * inner_mean) * inverse_rms + rows_grad.astype(jnp.float32)).astype(jnp.bfloat16)
        part_in = (jnp.dot(normed_b.T, grad_projected, preferred_element_type=jnp.float32) * grad_scale).astype(jnp.bfloat16)
        part_out = (jnp.dot(attention_output.T, rows_grad, preferred_element_type=jnp.float32) * grad_scale).astype(jnp.bfloat16)
        part_in = lax.optimization_barrier(part_in).astype(jnp.float32)
        part_out = lax.optimization_barrier(part_out).astype(jnp.float32)
        return ((carry[0] + part_in, carry[1] + part_out), (mixed_rows, grad_rows_in))
    start = (jnp.zeros((D, QKV_W), jnp.float32), jnp.zeros((QUERY_COLUMNS, D), jnp.float32))
    (sum_in, sum_out), (mixed, grad_hidden) = lax.scan(one_device, start, (hidden_rows, doc_ids, grad_rows))
    return (mixed.reshape(TOKENS, D), grad_hidden.reshape(TOKENS, D), sum_in.reshape(-1), sum_out.reshape(-1))
```

```python
import math

import jax
import jax.numpy as jnp
from jax import lax
from jax.experimental import pallas as pl
from jax.experimental.pallas import tpu as pltpu
from jax.sharding import PartitionSpec as P

MESH = pl.DeviceIdType.MESH
F32, BF16 = jnp.float32, jnp.bfloat16
D, HEADS, HS = 896, 7, 64
TOK = 128
NX, NZ, NY = 4, 16, 8
ROPE_BASE = 1000000.0
EPS = 1e-06
VMEM = pltpu.VMEM
NT = (((1,), (1,)), ((), ()))
TN = (((0,), (0,)), ((), ()))


def coords():
    o = lax.axis_index("outer")
    i = lax.axis_index("inner")
    return lax.div(o, 16), lax.rem(o, 16), lax.div(i, 2), lax.rem(i, 2)


def device(x, z, y, c):
    return (x * 16 + z, y * 2 + c)


def signal(sem, dev):
    pl.semaphore_signal(sem, inc=1, device_id=dev, device_id_type=MESH)


def remote(src, dst, send, recv, dev):
    return pltpu.make_async_remote_copy(
        src_ref=src, dst_ref=dst, send_sem=send, recv_sem=recv, device_id=dev, device_id_type=MESH
    )


def lanes(shape, dim=1):
    return lax.broadcasted_iota(jnp.int32, shape, dim)


def swap_halves(v):
    low = (lanes(v.shape) & 63) < 32
    return jnp.where(low, pltpu.roll(v, 96, 1), pltpu.roll(v, 32, 1))


def allowed_pairs(doc_ref):
    row = jnp.broadcast_to(doc_ref[...].astype(F32), (TOK, TOK))
    return (row == row.T) & (lanes((TOK, TOK)) <= lanes((TOK, TOK), 0))


def gather_kernel(
    codes_ref, scale_ref, hid_ref, doc_ref,
    w_ref, nb_ref, irms_ref, cos_ref, sin_ref,
    own, ysend, yrecv, csend, crecv, lsem,
):
    x, z, y, c = coords()
    me = 2 * y + c
    sib = device(x, z, y, 1 - c)
    peers = [lax.rem(y + k, NY) for k in range(1, NY)]
    barrier = pltpu.get_barrier_semaphore()
    signal(barrier, sib)
    for p in peers:
        signal(barrier, device(x, z, p, c))

    first = lax.div(7 * me, 4)
    start = 56 * me - 32 * first
    block = (lanes((56, 1024), 0) + start) >> 5
    s0 = scale_ref[pl.ds(first, 1), :]
    s1 = scale_ref[pl.ds(first + 1, 1), :]
    s2 = scale_ref[pl.ds(jnp.minimum(first + 2, 27), 1), :]
    scale = jnp.where(block == 0, s0, jnp.where(block == 1, s1, s2))
    own[...] = (codes_ref[...].astype(F32) * scale).astype(BF16)
    local = pltpu.make_async_copy(own, w_ref.at[me], lsem)
    local.start()
    pl.semaphore_wait(barrier, NY)
    copies = []
    for k, p in enumerate(peers):
        cp = remote(own, w_ref.at[me], ysend.at[k], yrecv.at[y], device(x, z, p, c))
        cp.start()
        copies.append(cp)
    cp = remote(own, w_ref.at[me], csend.at[y], crecv.at[y], sib)
    cp.start()
    copies.append(cp)

    rows = hid_ref[...].astype(F32)
    irms = lax.rsqrt(jnp.mean(rows * rows, axis=1, keepdims=True) + EPS)
    nb_ref[...] = (rows * irms).astype(BF16)
    irms_ref[...] = jnp.broadcast_to(irms, (TOK, 128))
    pos = jnp.sum(jnp.where(allowed_pairs(doc_ref), 1.0, 0.0), axis=1, keepdims=True) - 1.0
    lane = lanes((TOK, 128))
    freq = jnp.exp((lane & 31).astype(F32) * (-2.0 * math.log(ROPE_BASE) / HS))
    angle = pos * freq
    cos_ref[...] = jnp.cos(angle)
    sine = jnp.sin(angle)
    sin_ref[...] = jnp.where((lane & 63) < 32, -sine, sine)

    for p in peers:
        slot = w_ref.at[2 * p + c]
        remote(own, slot, ysend.at[0], yrecv.at[p], sib).wait_recv()
        cp = remote(slot, slot, csend.at[p], crecv.at[p], sib)
        cp.start()
        copies.append(cp)
    for p in range(NY):
        slot = w_ref.at[2 * p + 1 - c]
        remote(own, slot, csend.at[0], crecv.at[p], sib).wait_recv()
    for cp in copies:
        cp.wait_send()
    local.wait()


def main_kernel(
    w_ref, hid_ref, gm_ref, doc_ref, nb_ref, irms_ref, cos_ref, sin_ref,
    mixed_ref, gh_ref, gout_ref,
    mixbuf, ghbuf, pin, pout, cin, cout, xin, xout, xrin, xrout, ybuf, yrbuf, msg, rbuf,
    cs, cr, xs, xr, ys, yr, fs, fr, ls,
):
    x, z, y, c = coords()
    me = 2 * y + c
    sib = device(x, z, y, 1 - c)
    xpeers = [lax.rem(x + k, NX) for k in range(1, NX)]
    ypeers = [lax.rem(y + k, NY) for k in range(1, NY)]
    owner = 8 * c + y
    diagonal = z == owner
    barrier = pltpu.get_barrier_semaphore()
    signal(barrier, sib)
    for p in xpeers:
        signal(barrier, device(p, z, y, c))
    for p in ypeers:
        signal(barrier, device(x, z, p, c))
    sy, sc = lax.rem(z, 8), lax.div(z, 8)
    for k in range(1, NZ):
        signal(barrier, device(x, lax.rem(z + k, NZ), sy, sc))

    @pl.when(jnp.logical_not(diagonal))
    def _():
        signal(barrier, device(x, z, sy, sc))

    lo = lanes((TOK, 128)) < 64
    cos, sin = cos_ref[...], sin_ref[...]
    grad_scale = 131072 ** (-0.5)
    zero = jnp.zeros((TOK, 128), F32)

    proj = jnp.dot(nb_ref[...], w_ref[:, :640], preferred_element_type=F32)
    q = []
    for t in range(4):
        v = proj[:, 128 * t : 128 * t + 128]
        q.append(v * cos + swap_halves(v) * sin)
    k_hi = jnp.where(lo, zero, q[3])
    k_lo = pltpu.roll(k_hi, 64, 1)
    q[3] = jnp.where(lo, q[3], zero)
    qb = [v.astype(BF16) for v in q]
    kk = jnp.concatenate([k_lo.astype(BF16), k_hi.astype(BF16)], axis=0)
    v_lo = jnp.where(lo, proj[:, 512:640], zero)
    v_hi = pltpu.roll(v_lo, 64, 1)
    vv = jnp.concatenate([v_lo.astype(BF16), v_hi.astype(BF16)], axis=0)
    allowed = allowed_pairs(doc_ref)
    probs, pb = [], []
    for t in range(4):
        s2 = lax.dot_general(qb[t], kk if t < 3 else kk[:128], NT, preferred_element_type=F32)
        for h in range(2 if t < 3 else 1):
            s = jnp.where(allowed, s2[:, 128 * h : 128 * h + 128] * 0.125, -1e30)
            e = jnp.exp(s - jnp.max(s, axis=1, keepdims=True))
            p = e * (1.0 / jnp.sum(e, axis=1, keepdims=True))
            probs.append(p)
            pb.append(p.astype(BF16))
    att = [jnp.dot(pb[0], vv[128:], preferred_element_type=F32).astype(BF16)]
    for t in range(1, 4):
        pair = jnp.concatenate([pb[2 * t - 1], pb[2 * t]], axis=1)
        att.append(jnp.dot(pair, vv, preferred_element_type=F32).astype(BF16))
    a = jnp.concatenate(att, axis=1)
    gm = gm_ref[...]
    part = lax.dot_general(a, gm, TN, preferred_element_type=F32)
    for h in range(2):
        for p in range(NX):
            r = 64 + 112 * p + 56 * h
            pout[h, p] = (part[r : r + 56] * grad_scale).astype(BF16)
    pl.semaphore_wait(barrier, 27 - diagonal.astype(jnp.int32))
    copies = []
    for k in range(NX):
        p = lax.rem(x + 1 + k, NX)
        cp = remote(pout.at[1 - c, p], cout.at[p], cs.at[k], cr.at[p], sib)
        cp.start()
        copies.append(cp)

    ga = jnp.dot(gm, w_ref[:, 512:], preferred_element_type=F32)
    g = [ga[:, 128 * t : 128 * t + 128] for t in range(4)]
    g[0] = jnp.where(lo, zero, g[0])
    gb = [v.astype(BF16) for v in g]
    gs = [None] * 7
    for t in range(4):
        g2 = lax.dot_general(gb[t], vv if t > 0 else vv[128:], NT, preferred_element_type=F32)
        prod = gb[t].astype(F32) * att[t].astype(F32)
        for h in range(2 if t > 0 else 1):
            head = 2 * t - 1 + h if t > 0 else 0
            if t == 0:
                delta = jnp.sum(prod, axis=1, keepdims=True)
            else:
                delta = jnp.sum(jnp.where(lo, prod, zero) if h == 0 else jnp.where(lo, zero, prod), axis=1, keepdims=True)
            gp = g2[:, 128 * h : 128 * h + 128]
            gs[head] = (probs[head] * (gp - delta) * 0.125).astype(BF16)
    zb = jnp.zeros((TOK, 128), BF16)
    q_rows = [jnp.where(lo, q[h // 2], zero).astype(BF16) if h % 2 == 0 else jnp.where(lo, zero, q[h // 2]).astype(BF16) for h in range(7)]
    g_rows = [gb[0]] + [
        (jnp.where(lo, g[(h + 1) // 2], zero) if h % 2 == 1 else jnp.where(lo, zero, g[h // 2])).astype(BF16) for h in range(1, 7)
    ]
    gk = lax.dot_general(jnp.concatenate(gs, axis=0), jnp.concatenate(q_rows, axis=0), TN, preferred_element_type=F32)
    gk = gk + pltpu.roll(gk, 64, 1)
    gv = lax.dot_general(jnp.concatenate(pb, axis=0), jnp.concatenate(g_rows, axis=0), TN, preferred_element_type=F32)
    gv = gv + pltpu.roll(gv, 64, 1)
    tiles = []
    for t in range(4):
        if t < 3:
            pair = jnp.concatenate([gs[2 * t], gs[2 * t + 1]], axis=1)
            v = jnp.dot(pair, kk, preferred_element_type=F32)
        else:
            v = jnp.dot(gs[6], kk[:128], preferred_element_type=F32)
            v = jnp.where(lo, v, gk)
        tiles.append((v * cos - swap_halves(v) * sin).astype(BF16))
    tiles.append(jnp.where(lo, gv, zero).astype(BF16))
    gpa = jnp.concatenate(tiles, axis=1)
    part = lax.dot_general(nb_ref[...], gpa, TN, preferred_element_type=F32)
    for h in range(2):
        for p in range(NX):
            r = 224 * p + 112 * h
            pin[h, p] = (part[r : r + 112] * grad_scale).astype(BF16)
    for k in range(NX):
        p = lax.rem(x + 1 + k, NX)
        cp = remote(pin.at[1 - c, p], cin.at[p], cs.at[4 + k], cr.at[4 + p], sib)
        cp.start()
        copies.append(cp)

    sum_out = sum_in = None
    for k in range(NX):
        p = lax.rem(x + 1 + k, NX)
        remote(pout.at[c, p], cout.at[p], cs.at[0], cr.at[p], sib).wait_recv()
        s = pout[c, p].astype(F32) + cout[p].astype(F32)
        if k < NX - 1:
            xout[k] = s.astype(BF16)
            cp = remote(xout.at[k], xrout.at[x], xs.at[k], xr.at[x], device(p, z, y, c))
            cp.start()
            copies.append(cp)
        else:
            sum_out = s
    for k in range(NX):
        p = lax.rem(x + 1 + k, NX)
        remote(pin.at[c, p], cin.at[p], cs.at[0], cr.at[4 + p], sib).wait_recv()
        s = pin[c, p].astype(F32) + cin[p].astype(F32)
        if k < NX - 1:
            xin[k] = s.astype(BF16)
            cp = remote(xin.at[k], xrin.at[x], xs.at[4 + k], xr.at[4 + x], device(p, z, y, c))
            cp.start()
            copies.append(cp)
        else:
            sum_in = s

    out = lax.dot_general(a, w_ref[:, 512:], NT, preferred_element_type=F32)
    mixbuf[...] = (hid_ref[...].astype(F32) + out).astype(BF16)
    mix_copy = pltpu.make_async_copy(mixbuf, mixed_ref, ls.at[0])
    mix_copy.start()
    gn = lax.dot_general(gpa, w_ref[:, :640], NT, preferred_element_type=F32)
    irms = irms_ref[:, :1]
    normed = hid_ref[...].astype(F32) * irms
    mean = jnp.mean(gn * normed, axis=1, keepdims=True)
    ghbuf[...] = ((gn - normed * mean) * irms + gm.astype(F32)).astype(BF16)
    gh_copy = pltpu.make_async_copy(ghbuf, gh_ref, ls.at[1])
    gh_copy.start()

    for p in xpeers:
        remote(xout.at[0], xrout.at[p], xs.at[0], xr.at[p], sib).wait_recv()
        sum_out = sum_out + xrout[p].astype(F32)
    high = lanes((56, 512)) >= 64
    left = jnp.where(high, pltpu.roll(sum_out[:, :512], 64, 1), 0.0)
    right = jnp.where(high, sum_out[:, 384:], 0.0)
    halves = jnp.concatenate([left, right], axis=0).astype(BF16)
    row, col = lanes((128, 112), 0), lanes((128, 112))
    j = row & 7
    q7 = 7 * ((row >> 3) & 1) + j
    pick_out = (j < 7) & (col == 7 * (row >> 4) + (q7 >> 1) + 56 * (q7 & 1))
    pick_in = (j < 7) & (col == 7 * (row >> 3) + j)
    e_out = jnp.where(pick_out, 1.0, 0.0).astype(BF16)
    e_in = jnp.where(pick_in, 1.0, 0.0).astype(BF16)
    y_out = jnp.dot(e_out, halves, preferred_element_type=F32)
    for p in xpeers:
        remote(xin.at[0], xrin.at[p], xs.at[0], xr.at[4 + p], sib).wait_recv()
        sum_in = sum_in + xrin[p].astype(F32)
    y_in = jnp.dot(e_in, sum_in.astype(BF16), preferred_element_type=F32)
    for p in range(NY):
        rows = slice(16 * p, 16 * p + 16)
        ybuf[p, :, :512] = y_in[rows, :512].astype(BF16)
        ybuf[p, :, 512:640] = (y_in[rows, 512:] + y_out[rows, :128]).astype(BF16)
        ybuf[p, :, 640:] = y_out[rows, 128:].astype(BF16)
    for k, p in enumerate(ypeers):
        cp = remote(ybuf.at[p], yrbuf.at[y], ys.at[k], yr.at[y], device(x, z, p, c))
        cp.start()
        copies.append(cp)
    total = ybuf[y].astype(F32)
    for p in ypeers:
        remote(ybuf.at[0], yrbuf.at[p], ys.at[0], yr.at[p], sib).wait_recv()
        total = total + yrbuf[p].astype(F32)

    before = pltpu.roll(total, 1, 0)
    lane = lanes((16, 1024))
    jrow = lanes((16, 1024), 0) & 7
    flat = jnp.zeros((16, 1024), F32)
    for k in range(8):
        here = jnp.where(lane < 504, pltpu.roll(total, 72 * k, 1), pltpu.roll(total, (56 * k - 72) % 1024, 1))
        past = jnp.where(lane < 504, pltpu.roll(before, (448 + 72 * k) % 1024, 1), pltpu.roll(before, (504 + 56 * k) % 1024, 1))
        old = (lane < 72 * k) | ((lane >= 504) & (lane < 504 + 56 * k))
        flat = jnp.where(jrow == k, jnp.where(old, past, here), flat)
    for t in range(8):
        msg[:, t, :] = flat[:, 128 * t : 128 * t + 128]
    for k in range(1, 16):
        i = lax.rem(me + k, 16)
        cp = remote(msg.at[i], rbuf.at[z], fs.at[k], fr.at[z], device(x, owner, lax.div(i, 2), lax.rem(i, 2)))
        cp.start()
        copies.append(cp)
    mine = remote(msg.at[me], rbuf.at[z], fs.at[0], fr.at[z], device(x, owner, y, c))
    kept = pltpu.make_async_copy(msg.at[me], rbuf.at[z], ls.at[2])

    @pl.when(diagonal)
    def _():
        kept.start()
        kept.wait()

    @pl.when(jnp.logical_not(diagonal))
    def _():
        mine.start()
        mine.wait_send()
        remote(msg.at[0], rbuf.at[z], fs.at[0], fr.at[z], sib).wait_recv()

    for k in range(1, 16):
        s = lax.rem(z + k, 16)
        remote(msg.at[0], rbuf.at[s], fs.at[0], fr.at[s], sib).wait_recv()
    gout_ref[...] = jnp.sum(rbuf[...], axis=0)
    for cp in copies:
        cp.wait_send()
    mix_copy.wait()
    gh_copy.wait()


def body(hidden_in, doc_ids, grad_mixed, in_codes, in_scales, out_codes, out_scales):
    codes = jnp.concatenate([in_codes, out_codes.T], axis=1)
    scales = jnp.repeat(jnp.concatenate([in_scales, out_scales.T], axis=1), HS, axis=1)
    vm = pl.BlockSpec(memory_space=VMEM)
    anyspace = pl.BlockSpec(memory_space=pl.ANY)
    dma = pltpu.SemaphoreType.DMA
    sds = jax.ShapeDtypeStruct
    w, nb, irms, cos, sin = pl.pallas_call(
        gather_kernel,
        out_shape=(
            sds((16, 56, 1024), BF16), sds((TOK, D), BF16), sds((TOK, 128), F32),
            sds((TOK, 128), F32), sds((TOK, 128), F32),
        ),
        in_specs=[vm] * 4,
        out_specs=(anyspace, vm, vm, vm, vm),
        scratch_shapes=[VMEM((56, 1024), BF16), dma((7,)), dma((8,)), dma((8,)), dma((8,)), dma],
        compiler_params=pltpu.CompilerParams(collective_id=0, has_side_effects=True, vmem_limit_bytes=16 << 20),
        name="gather",
    )(codes, scales, hidden_in, doc_ids)
    mixed, grad_hidden, grads = pl.pallas_call(
        main_kernel,
        out_shape=(sds((TOK, D), BF16), sds((TOK, D), BF16), sds((8, 128), F32)),
        in_specs=[vm] * 8,
        out_specs=(anyspace, anyspace, vm),
        scratch_shapes=[
            VMEM((TOK, D), BF16), VMEM((TOK, D), BF16),
            VMEM((2, 4, 112, 640), BF16), VMEM((2, 4, 56, 896), BF16),
            VMEM((4, 112, 640), BF16), VMEM((4, 56, 896), BF16),
            VMEM((3, 112, 640), BF16), VMEM((3, 56, 896), BF16),
            VMEM((4, 112, 640), BF16), VMEM((4, 56, 896), BF16),
            VMEM((8, 16, 1024), BF16), VMEM((8, 16, 1024), BF16),
            VMEM((16, 8, 128), F32), VMEM((16, 8, 128), F32),
            dma((8,)), dma((8,)), dma((8,)), dma((8,)), dma((7,)), dma((8,)), dma((16,)), dma((16,)), dma((3,)),
        ],
        compiler_params=pltpu.CompilerParams(collective_id=1, has_side_effects=True, vmem_limit_bytes=32 << 20),
        name="sublayer",
    )(w.reshape(D, 1024), hidden_in, grad_mixed, doc_ids, nb, irms, cos, sin)
    flat = grads.reshape(1024)
    return mixed, grad_hidden, flat[:504], flat[504:896]


def solution(mesh):
    rows = P(("outer", "inner"), None)
    return jax.shard_map(
        body,
        mesh=mesh,
        in_specs=(rows, rows, rows, P("inner", None), P(), P(None, "inner"), P()),
        out_specs=(rows, rows, P(("outer", "inner")), P(("outer", "inner"))),
        check_vma=False,
    )
```

```python
import math

import jax
import jax.numpy as jnp
from jax import lax
from jax.experimental import pallas as pl
from jax.experimental.pallas import tpu as pltpu
from jax.sharding import PartitionSpec as P

MESH = pl.DeviceIdType.MESH
F32, BF16 = jnp.float32, jnp.bfloat16
D, HEADS, HS = 896, 7, 64
TOK = 128
NX, NZ, NY = 4, 16, 8
ROPE_BASE = 1000000.0
EPS = 1e-06
VMEM = pltpu.VMEM
NT = (((1,), (1,)), ((), ()))
TN = (((0,), (0,)), ((), ()))


def coords():
    o = lax.axis_index("outer")
    i = lax.axis_index("inner")
    return lax.div(o, 16), lax.rem(o, 16), lax.div(i, 2), lax.rem(i, 2)


def device(x, z, y, c):
    return (x * 16 + z, y * 2 + c)


def signal(sem, dev):
    pl.semaphore_signal(sem, inc=1, device_id=dev, device_id_type=MESH)


def remote(src, dst, send, recv, dev):
    return pltpu.make_async_remote_copy(
        src_ref=src, dst_ref=dst, send_sem=send, recv_sem=recv, device_id=dev, device_id_type=MESH
    )


def lanes(shape, dim=1):
    return lax.broadcasted_iota(jnp.int32, shape, dim)


def swap_halves(v):
    low = (lanes(v.shape) & 63) < 32
    return jnp.where(low, pltpu.roll(v, 96, 1), pltpu.roll(v, 32, 1))


def allowed_pairs(doc_ref):
    row = jnp.broadcast_to(doc_ref[...].astype(F32), (TOK, TOK))
    return (row == row.T) & (lanes((TOK, TOK)) <= lanes((TOK, TOK), 0))


def gather_kernel(
    inc_ref, outc_ref, ins_ref, outs_ref, hid_ref, doc_ref,
    w_ref, nb_ref, irms_ref, cos_ref, sin_ref, mask_ref,
    ic, oc, ins, outs, hid, doc, pad, lsem, ysend, yrecv, xsend, xrecv, csend, crecv,
):
    x, z, y, c = coords()
    me = 2 * y + c
    sib = device(x, z, y, 1 - c)
    xpeers = [lax.rem(x + k, NX) for k in (1, 3, 2)]
    ypeers = [lax.rem(y + k, NY) for k in (1, 7, 2, 6, 3, 5, 4)]
    barrier = pltpu.get_barrier_semaphore()
    for p in ypeers:
        signal(barrier, device(x, z, p, c))
    for p in xpeers:
        signal(barrier, device(p, z, y, c))
    signal(barrier, sib)
    pairs = ((inc_ref, ic), (outc_ref, oc), (ins_ref, ins), (outs_ref, outs), (doc_ref, doc), (hid_ref, hid))
    loads = [pltpu.make_async_copy(src, dst, lsem.at[k]) for k, (src, dst) in enumerate(pairs)]
    for cp in loads:
        cp.start()
    pad[...] = jnp.zeros((56, 128), F32)
    for cp in loads[:4]:
        cp.wait()

    shift = jnp.where(lanes((448, 512)) == lanes((448, 512), 0) + 64, 1.0, 0.0).astype(BF16)
    turned = jnp.dot(oc[...], shift, preferred_element_type=F32)
    block = (lanes((56, 28), 0) + 56 * me) >> 5
    pick = jnp.where(block == lanes((56, 28)), 1.0, 0.0)
    s_in = lax.dot_general(pick, ins[...], NT, precision=lax.Precision.HIGHEST, preferred_element_type=F32)
    s_out = lax.dot_general(pick, outs[...], NT, precision=lax.Precision.HIGHEST, preferred_element_type=F32)
    columns = [s_in[:, k : k + 1] for k in range(9)] + [s_out[:, k : k + 1] for k in range(7)]
    low = lanes((56, 128)) < 64
    pad[:, :64] = ic[:, 512:].astype(F32)
    for t in range(8):
        if t < 4:
            code = ic[:, 128 * t : 128 * t + 128].astype(F32)
        else:
            code = turned[:, 128 * t - 512 : 128 * t - 384]
            if t == 4:
                code = code + pad[...]
        scale = jnp.where(low, columns[2 * t], columns[2 * t + 1])
        w_ref[t // 2, y, c, :, 128 * (t % 2) : 128 * (t % 2) + 128] = (code * scale).astype(BF16)

    pl.semaphore_wait(barrier, 11)
    mine = w_ref.at[x, y, c]
    for k, p in enumerate(ypeers):
        remote(mine, mine, ysend, yrecv.at[y], device(x, z, p, c)).start()
    whole = w_ref.at[:, y, c]
    remote(whole, whole, csend, crecv, sib).start()

    loads[4].wait()
    loads[5].wait()
    rows = hid[...].astype(F32)
    irms = lax.rsqrt(jnp.mean(rows * rows, axis=1, keepdims=True) + EPS)
    nb_ref[...] = (rows * irms).astype(BF16)
    irms_ref[...] = jnp.broadcast_to(irms, (TOK, 128))
    mask = jnp.where(allowed_pairs(doc), 1.0, 0.0)
    mask_ref[...] = mask
    pos = jnp.sum(mask, axis=1, keepdims=True) - 1.0
    lane = lanes((TOK, 128))
    freq = jnp.exp((lane & 31).astype(F32) * (-2.0 * math.log(ROPE_BASE) / HS))
    angle = pos * freq
    cos_ref[...] = jnp.cos(angle)
    sine = jnp.sin(angle)
    sin_ref[...] = jnp.where((lane & 63) < 32, -sine, sine)

    def onward(p):
        for q in xpeers:
            piece = w_ref.at[q, p, c]
            remote(piece, piece, xsend, xrecv.at[q, p], sib).wait_recv()
        row = w_ref.at[:, p, c]
        remote(row, row, csend, crecv, sib).start()

    for n, p in enumerate(ypeers):
        piece = w_ref.at[x, p, c]
        remote(piece, piece, ysend, yrecv.at[p], sib).wait_recv()
        for q in xpeers:
            remote(piece, piece, xsend, xrecv.at[x, p], device(q, z, y, c)).start()
        if n >= 2:
            onward(ypeers[n - 2])
    onward(ypeers[5])
    onward(ypeers[6])
    half = w_ref.at[:, pl.ds(0, 4)]
    remote(half, half, csend, crecv, sib).wait()
    seven = w_ref.at[0, pl.ds(0, 7), 0]
    remote(seven, seven, ysend, yrecv.at[0], sib).wait_send()
    more = w_ref.at[pl.ds(0, 3), pl.ds(0, 7), 0]
    remote(more, more, xsend, yrecv.at[0], sib).wait_send()


def main_kernel(
    w_ref, hid_hbm, gm_hbm, nb_ref, irms_ref, cos_ref, sin_ref, mask_ref,
    mixed_ref, gh_ref, gout_ref,
    hid_ref, gm_ref, pin, pout, cin, cout, xin, xout, xrin, xrout, ybuf, yrbuf, msg, rbuf,
    cs, cr, xs, xr, ys, yr, fs, fr, ls,
):
    x, z, y, c = coords()
    me = 2 * y + c
    sib = device(x, z, y, 1 - c)
    xpeers = [lax.rem(x + k, NX) for k in range(1, NX)]
    ypeers = [lax.rem(y + k, NY) for k in range(1, NY)]
    owner = 8 * c + y
    diagonal = z == owner
    barrier = pltpu.get_barrier_semaphore()
    signal(barrier, sib)
    for p in xpeers:
        signal(barrier, device(p, z, y, c))
    for p in ypeers:
        signal(barrier, device(x, z, p, c))
    sy, sc = lax.rem(z, 8), lax.div(z, 8)
    for k in range(1, NZ):
        signal(barrier, device(x, lax.rem(z + k, NZ), sy, sc))

    @pl.when(jnp.logical_not(diagonal))
    def _():
        signal(barrier, device(x, z, sy, sc))

    gm_load = pltpu.make_async_copy(gm_hbm, gm_ref, ls.at[0])
    gm_load.start()
    hid_load = pltpu.make_async_copy(hid_hbm, hid_ref, ls.at[1])
    hid_load.start()

    lo = lanes((TOK, 128)) < 64
    cos, sin = cos_ref[...], sin_ref[...]
    grad_scale = 131072 ** (-0.5)
    zero = jnp.zeros((TOK, 128), F32)

    nb = nb_ref[...]
    proj = [jnp.dot(nb, w_ref[t], preferred_element_type=F32) for t in range(2)]
    proj.append(jnp.dot(nb, w_ref[2, :, :128], preferred_element_type=F32))
    q = []
    for t in range(4):
        v = proj[t // 2][:, 128 * (t % 2) : 128 * (t % 2) + 128]
        q.append(v * cos + swap_halves(v) * sin)
    k_hi = jnp.where(lo, zero, q[3])
    k_lo = pltpu.roll(k_hi, 64, 1)
    q[3] = jnp.where(lo, q[3], zero)
    qb = [v.astype(BF16) for v in q]
    kk = jnp.concatenate([k_lo.astype(BF16), k_hi.astype(BF16)], axis=0)
    v_lo = jnp.where(lo, proj[2], zero)
    v_hi = pltpu.roll(v_lo, 64, 1)
    vv = jnp.concatenate([v_lo.astype(BF16), v_hi.astype(BF16)], axis=0)
    allowed = mask_ref[...] > 0.5
    probs, pb = [], []
    for t in range(4):
        s2 = lax.dot_general(qb[t], kk if t < 3 else kk[:128], NT, preferred_element_type=F32)
        for h in range(2 if t < 3 else 1):
            s = jnp.where(allowed, s2[:, 128 * h : 128 * h + 128] * 0.125, -1e30)
            e = jnp.exp(s - jnp.max(s, axis=1, keepdims=True))
            p = e * (1.0 / jnp.sum(e, axis=1, keepdims=True))
            probs.append(p)
            pb.append(p.astype(BF16))
    att = [jnp.dot(pb[0], vv[128:], preferred_element_type=F32).astype(BF16)]
    for t in range(1, 4):
        pair = jnp.concatenate([pb[2 * t - 1], pb[2 * t]], axis=1)
        att.append(jnp.dot(pair, vv, preferred_element_type=F32).astype(BF16))
    a = jnp.concatenate(att, axis=1)
    gm_load.wait()
    gm = gm_ref[...]
    part = lax.dot_general(a, gm, TN, preferred_element_type=F32)
    for h in range(2):
        for p in range(NX):
            r = 64 + 112 * p + 56 * h
            pout[h, p] = (part[r : r + 56] * grad_scale).astype(BF16)
    pl.semaphore_wait(barrier, 27 - diagonal.astype(jnp.int32))
    copies = []
    for k in range(NX):
        p = lax.rem(x + 1 + k, NX)
        cp = remote(pout.at[1 - c, p], cout.at[p], cs.at[k], cr.at[p], sib)
        cp.start()
        copies.append(cp)

    ga = [jnp.dot(gm, w_ref[t], preferred_element_type=F32) for t in (2, 3)]
    g = [ga[t // 2][:, 128 * (t % 2) : 128 * (t % 2) + 128] for t in range(4)]
    g[0] = jnp.where(lo, zero, g[0])
    gb = [v.astype(BF16) for v in g]
    gs = [None] * 7
    for t in range(4):
        g2 = lax.dot_general(gb[t], vv if t > 0 else vv[128:], NT, preferred_element_type=F32)
        prod = gb[t].astype(F32) * att[t].astype(F32)
        for h in range(2 if t > 0 else 1):
            head = 2 * t - 1 + h if t > 0 else 0
            if t == 0:
                delta = jnp.sum(prod, axis=1, keepdims=True)
            else:
                delta = jnp.sum(jnp.where(lo, prod, zero) if h == 0 else jnp.where(lo, zero, prod), axis=1, keepdims=True)
            gp = g2[:, 128 * h : 128 * h + 128]
            gs[head] = (probs[head] * (gp - delta) * 0.125).astype(BF16)
    zb = jnp.zeros((TOK, 128), BF16)
    q_rows = [jnp.where(lo, q[h // 2], zero).astype(BF16) if h % 2 == 0 else jnp.where(lo, zero, q[h // 2]).astype(BF16) for h in range(7)]
    g_rows = [gb[0]] + [
        (jnp.where(lo, g[(h + 1) // 2], zero) if h % 2 == 1 else jnp.where(lo, zero, g[h // 2])).astype(BF16) for h in range(1, 7)
    ]
    gk = lax.dot_general(jnp.concatenate(gs, axis=0), jnp.concatenate(q_rows, axis=0), TN, preferred_element_type=F32)
    gk = gk + pltpu.roll(gk, 64, 1)
    gv = lax.dot_general(jnp.concatenate(pb, axis=0), jnp.concatenate(g_rows, axis=0), TN, preferred_element_type=F32)
    gv = gv + pltpu.roll(gv, 64, 1)
    tiles = []
    for t in range(4):
        if t < 3:
            pair = jnp.concatenate([gs[2 * t], gs[2 * t + 1]], axis=1)
            v = jnp.dot(pair, kk, preferred_element_type=F32)
        else:
            v = jnp.dot(gs[6], kk[:128], preferred_element_type=F32)
            v = jnp.where(lo, v, gk)
        tiles.append((v * cos - swap_halves(v) * sin).astype(BF16))
    tiles.append(jnp.where(lo, gv, zero).astype(BF16))
    gpa = jnp.concatenate(tiles, axis=1)
    part = lax.dot_general(nb, gpa, TN, preferred_element_type=F32)
    for h in range(2):
        for p in range(NX):
            r = 224 * p + 112 * h
            pin[h, p] = (part[r : r + 112] * grad_scale).astype(BF16)
    for k in range(NX):
        p = lax.rem(x + 1 + k, NX)
        cp = remote(pin.at[1 - c, p], cin.at[p], cs.at[4 + k], cr.at[4 + p], sib)
        cp.start()
        copies.append(cp)

    sum_out = sum_in = None
    for k in range(NX):
        p = lax.rem(x + 1 + k, NX)
        remote(pout.at[c, p], cout.at[p], cs.at[0], cr.at[p], sib).wait_recv()
        s = pout[c, p].astype(F32) + cout[p].astype(F32)
        if k < NX - 1:
            xout[k] = s.astype(BF16)
            cp = remote(xout.at[k], xrout.at[x], xs.at[k], xr.at[x], device(p, z, y, c))
            cp.start()
            copies.append(cp)
        else:
            sum_out = s
    for k in range(NX):
        p = lax.rem(x + 1 + k, NX)
        remote(pin.at[c, p], cin.at[p], cs.at[0], cr.at[4 + p], sib).wait_recv()
        s = pin[c, p].astype(F32) + cin[p].astype(F32)
        if k < NX - 1:
            xin[k] = s.astype(BF16)
            cp = remote(xin.at[k], xrin.at[x], xs.at[4 + k], xr.at[4 + x], device(p, z, y, c))
            cp.start()
            copies.append(cp)
        else:
            sum_in = s

    hid_load.wait()
    hid = hid_ref[...].astype(F32)
    out = sum(lax.dot_general(a[:, 256 * t : 256 * t + 256], w_ref[2 + t], NT, preferred_element_type=F32) for t in range(2))
    mixed_ref[...] = (hid + out).astype(BF16)
    gn = sum(lax.dot_general(gpa[:, 256 * t : 256 * t + 256], w_ref[t], NT, preferred_element_type=F32) for t in range(2))
    gn = gn + lax.dot_general(gpa[:, 512:], w_ref[2, :, :128], NT, preferred_element_type=F32)
    irms = irms_ref[:, :1]
    normed = hid * irms
    mean = jnp.mean(gn * normed, axis=1, keepdims=True)
    gh_ref[...] = ((gn - normed * mean) * irms + gm.astype(F32)).astype(BF16)

    for p in xpeers:
        remote(xout.at[0], xrout.at[p], xs.at[0], xr.at[p], sib).wait_recv()
        sum_out = sum_out + xrout[p].astype(F32)
    high = lanes((56, 512)) >= 64
    left = jnp.where(high, pltpu.roll(sum_out[:, :512], 64, 1), 0.0)
    right = jnp.where(high, sum_out[:, 384:], 0.0)
    halves = jnp.concatenate([left, right], axis=0).astype(BF16)
    row, col = lanes((128, 112), 0), lanes((128, 112))
    j = row & 7
    q7 = 7 * ((row >> 3) & 1) + j
    pick_out = (j < 7) & (col == 7 * (row >> 4) + (q7 >> 1) + 56 * (q7 & 1))
    pick_in = (j < 7) & (col == 7 * (row >> 3) + j)
    e_out = jnp.where(pick_out, 1.0, 0.0).astype(BF16)
    e_in = jnp.where(pick_in, 1.0, 0.0).astype(BF16)
    y_out = jnp.dot(e_out, halves, preferred_element_type=F32)
    for p in xpeers:
        remote(xin.at[0], xrin.at[p], xs.at[0], xr.at[4 + p], sib).wait_recv()
        sum_in = sum_in + xrin[p].astype(F32)
    y_in = jnp.dot(e_in, sum_in.astype(BF16), preferred_element_type=F32)
    for p in range(NY):
        rows = slice(16 * p, 16 * p + 16)
        ybuf[p, :, :512] = y_in[rows, :512].astype(BF16)
        ybuf[p, :, 512:640] = (y_in[rows, 512:] + y_out[rows, :128]).astype(BF16)
        ybuf[p, :, 640:] = y_out[rows, 128:].astype(BF16)
    for k, p in enumerate(ypeers):
        cp = remote(ybuf.at[p], yrbuf.at[y], ys.at[k], yr.at[y], device(x, z, p, c))
        cp.start()
        copies.append(cp)
    total = ybuf[y].astype(F32)
    for p in ypeers:
        remote(ybuf.at[0], yrbuf.at[p], ys.at[0], yr.at[p], sib).wait_recv()
        total = total + yrbuf[p].astype(F32)

    before = pltpu.roll(total, 1, 0)
    lane = lanes((16, 1024))
    jrow = lanes((16, 1024), 0) & 7
    flat = jnp.zeros((16, 1024), F32)
    for k in range(8):
        here = jnp.where(lane < 504, pltpu.roll(total, 72 * k, 1), pltpu.roll(total, (56 * k - 72) % 1024, 1))
        past = jnp.where(lane < 504, pltpu.roll(before, (448 + 72 * k) % 1024, 1), pltpu.roll(before, (504 + 56 * k) % 1024, 1))
        old = (lane < 72 * k) | ((lane >= 504) & (lane < 504 + 56 * k))
        flat = jnp.where(jrow == k, jnp.where(old, past, here), flat)
    for t in range(8):
        msg[:, t, :] = flat[:, 128 * t : 128 * t + 128]
    for k in range(1, 16):
        i = lax.rem(me + k, 16)
        cp = remote(msg.at[i], rbuf.at[z], fs.at[k], fr.at[z], device(x, owner, lax.div(i, 2), lax.rem(i, 2)))
        cp.start()
        copies.append(cp)
    mine = remote(msg.at[me], rbuf.at[z], fs.at[0], fr.at[z], device(x, owner, y, c))
    kept = pltpu.make_async_copy(msg.at[me], rbuf.at[z], ls.at[2])

    @pl.when(diagonal)
    def _():
        kept.start()
        kept.wait()

    @pl.when(jnp.logical_not(diagonal))
    def _():
        mine.start()
        mine.wait_send()
        remote(msg.at[0], rbuf.at[z], fs.at[0], fr.at[z], sib).wait_recv()

    for k in range(1, 16):
        s = lax.rem(z + k, 16)
        remote(msg.at[0], rbuf.at[s], fs.at[0], fr.at[s], sib).wait_recv()
    total = jnp.sum(rbuf[...], axis=0)
    for t in range(8):
        gout_ref[:, 128 * t : 128 * t + 128] = total[t : t + 1]
    for cp in copies:
        cp.wait_send()


def write_kernel(mixed_ref, gh_ref, grads_ref, mixed_out, gh_out, in_out, out_out, sem):
    copies = [pltpu.make_async_copy(mixed_ref, mixed_out, sem.at[0]), pltpu.make_async_copy(gh_ref, gh_out, sem.at[1])]
    for cp in copies:
        cp.start()
    flat = grads_ref[...]
    in_out[...] = flat[:, :504]
    out_out[...] = pltpu.roll(flat, 520, 1)[:, :392]
    for cp in copies:
        cp.wait()


def body(hidden_in, doc_ids, grad_mixed, in_codes, in_scales, out_codes, out_scales):
    vm = pl.BlockSpec(memory_space=VMEM)
    hbm = pl.BlockSpec(memory_space=pltpu.HBM)
    dma = pltpu.SemaphoreType.DMA
    sds = jax.ShapeDtypeStruct
    tokens = sds((TOK, D), BF16)
    square = sds((TOK, 128), F32)
    held = [pltpu.with_memory_space_constraint(v, pltpu.HBM) for v in (in_codes, out_codes.T, in_scales.T, out_scales, hidden_in, doc_ids)]
    grad_mixed = pltpu.with_memory_space_constraint(grad_mixed, pltpu.HBM)
    w, nb, irms, cos, sin, mask = pl.pallas_call(
        gather_kernel,
        out_shape=(sds((4, 8, 2, 56, 256), BF16), tokens, square, square, square, square),
        in_specs=[hbm] * 6,
        out_specs=(vm,) * 6,
        scratch_shapes=[
            VMEM((56, 576), BF16), VMEM((56, 448), BF16), VMEM((9, 28), F32), VMEM((7, 28), F32),
            VMEM((TOK, D), BF16), VMEM((1, 128), jnp.int32), VMEM((56, 128), F32),
            dma((6,)), dma, dma((8,)), dma, dma((4, 8)), dma, dma,
        ],
        compiler_params=pltpu.CompilerParams(collective_id=0, has_side_effects=True, vmem_limit_bytes=16 << 20),
        name="gather",
    )(*held)
    mixed, grad_hidden, grads = pl.pallas_call(
        main_kernel,
        out_shape=(tokens, tokens, sds((1, 1024), F32)),
        in_specs=[vm, hbm, hbm] + [vm] * 5,
        out_specs=(vm, vm, vm),
        scratch_shapes=[
            VMEM((TOK, D), BF16), VMEM((TOK, D), BF16),
            VMEM((2, 4, 112, 640), BF16), VMEM((2, 4, 56, 896), BF16),
            VMEM((4, 112, 640), BF16), VMEM((4, 56, 896), BF16),
            VMEM((3, 112, 640), BF16), VMEM((3, 56, 896), BF16),
            VMEM((4, 112, 640), BF16), VMEM((4, 56, 896), BF16),
            VMEM((8, 16, 1024), BF16), VMEM((8, 16, 1024), BF16),
            VMEM((16, 8, 128), F32), VMEM((16, 8, 128), F32),
            dma((8,)), dma((8,)), dma((8,)), dma((8,)), dma((7,)), dma((8,)), dma((16,)), dma((16,)), dma((3,)),
        ],
        compiler_params=pltpu.CompilerParams(collective_id=1, has_side_effects=True, vmem_limit_bytes=32 << 20),
        name="sublayer",
    )(w.reshape(4, D, 256), held[4], grad_mixed, nb, irms, cos, sin, mask)
    mixed, grad_hidden, grad_in, grad_out = pl.pallas_call(
        write_kernel,
        out_shape=(pltpu.HBM((TOK, D), BF16), pltpu.HBM((TOK, D), BF16), pltpu.HBM((1, 504), F32), pltpu.HBM((1, 392), F32)),
        in_specs=[vm] * 3,
        out_specs=(hbm, hbm, pl.BlockSpec(), pl.BlockSpec()),
        scratch_shapes=[dma((2,))],
        name="write",
    )(*(pltpu.with_memory_space_constraint(v, VMEM) for v in (mixed, grad_hidden, grads)))
    return mixed, grad_hidden, grad_in.reshape(504), grad_out.reshape(392)


def solution(mesh):
    rows = P(("outer", "inner"), None)
    return jax.shard_map(
        body,
        mesh=mesh,
        in_specs=(rows, rows, rows, P("inner", None), P(), P(None, "inner"), P()),
        out_specs=(rows, rows, P(("outer", "inner")), P(("outer", "inner"))),
        check_vma=False,
    )
```

```python
import math

import jax
import jax.numpy as jnp
from jax import lax
from jax.experimental import pallas as pl
from jax.experimental.pallas import tpu as pltpu
from jax.sharding import PartitionSpec as P

MESH = pl.DeviceIdType.MESH
F32, BF16 = jnp.float32, jnp.bfloat16
D, HEADS, HS = 896, 7, 64
TOK = 128
NX, NZ, NY = 4, 16, 8
ROPE_BASE = 1000000.0
EPS = 1e-06
VMEM = pltpu.VMEM
NT = (((1,), (1,)), ((), ()))
TN = (((0,), (0,)), ((), ()))


def coords():
    o = lax.axis_index("outer")
    i = lax.axis_index("inner")
    return lax.div(o, 16), lax.rem(o, 16), lax.div(i, 2), lax.rem(i, 2)


def device(x, z, y, c):
    return (x * 16 + z, y * 2 + c)


def signal(sem, dev):
    pl.semaphore_signal(sem, inc=1, device_id=dev, device_id_type=MESH)


def remote(src, dst, send, recv, dev):
    return pltpu.make_async_remote_copy(
        src_ref=src, dst_ref=dst, send_sem=send, recv_sem=recv, device_id=dev, device_id_type=MESH
    )


def lanes(shape, dim=1):
    return lax.broadcasted_iota(jnp.int32, shape, dim)


def swap_halves(v):
    low = (lanes(v.shape) & 63) < 32
    return jnp.where(low, pltpu.roll(v, 96, 1), pltpu.roll(v, 32, 1))


def allowed_pairs(doc_ref):
    row = jnp.broadcast_to(doc_ref[...].astype(F32), (TOK, TOK))
    return (row == row.T) & (lanes((TOK, TOK)) <= lanes((TOK, TOK), 0))


def gather_kernel(
    inc_ref, outc_ref, ins_ref, outs_ref, hid_ref, doc_ref,
    w_ref, nb_ref, irms_ref, cos_ref, sin_ref, mask_ref,
    ic, oc, ins, outs, hid, doc, pad, lsem, ysend, yrecv, xsend, xrecv, csend, crecv,
):
    x, z, y, c = coords()
    me = 2 * y + c
    sib = device(x, z, y, 1 - c)
    xpeers = [lax.rem(x + k, NX) for k in (1, 3, 2)]
    ypeers = [lax.rem(y + k, NY) for k in (1, 7, 2, 6, 3, 5, 4)]
    barrier = pltpu.get_barrier_semaphore()
    for p in ypeers:
        signal(barrier, device(x, z, p, c))
    for p in xpeers:
        signal(barrier, device(p, z, y, c))
    signal(barrier, sib)
    pairs = ((inc_ref, ic), (outc_ref, oc), (ins_ref, ins), (outs_ref, outs), (doc_ref, doc), (hid_ref, hid))
    loads = [pltpu.make_async_copy(src, dst, lsem.at[k]) for k, (src, dst) in enumerate(pairs)]
    for cp in loads:
        cp.start()
    pad[...] = jnp.zeros((56, 128), F32)
    for cp in loads[:4]:
        cp.wait()

    shift = jnp.where(lanes((448, 512)) == lanes((448, 512), 0) + 64, 1.0, 0.0).astype(BF16)
    turned = jnp.dot(oc[...], shift, preferred_element_type=F32)
    block = (lanes((56, 28), 0) + 56 * me) >> 5
    pick = jnp.where(block == lanes((56, 28)), 1.0, 0.0)
    s_in = lax.dot_general(pick, ins[...], NT, precision=lax.Precision.HIGHEST, preferred_element_type=F32)
    s_out = lax.dot_general(pick, outs[...], NT, precision=lax.Precision.HIGHEST, preferred_element_type=F32)
    columns = [s_in[:, k : k + 1] for k in range(9)] + [s_out[:, k : k + 1] for k in range(7)]
    low = lanes((56, 128)) < 64
    pad[:, :64] = ic[:, 512:].astype(F32)
    for t in range(8):
        if t < 4:
            code = ic[:, 128 * t : 128 * t + 128].astype(F32)
        else:
            code = turned[:, 128 * t - 512 : 128 * t - 384]
            if t == 4:
                code = code + pad[...]
        scale = jnp.where(low, columns[2 * t], columns[2 * t + 1])
        w_ref[t // 2, y, c, :, 128 * (t % 2) : 128 * (t % 2) + 128] = (code * scale).astype(BF16)

    pl.semaphore_wait(barrier, 11)
    mine = w_ref.at[x, y, c]
    for k, p in enumerate(ypeers):
        remote(mine, mine, ysend, yrecv.at[y], device(x, z, p, c)).start()
    whole = w_ref.at[:, y, c]
    remote(whole, whole, csend, crecv, sib).start()

    loads[4].wait()
    loads[5].wait()
    rows = hid[...].astype(F32)
    irms = lax.rsqrt(jnp.mean(rows * rows, axis=1, keepdims=True) + EPS)
    nb_ref[...] = (rows * irms).astype(BF16)
    irms_ref[...] = jnp.broadcast_to(irms, (TOK, 128))
    mask = jnp.where(allowed_pairs(doc), 1.0, 0.0)
    mask_ref[...] = mask
    pos = jnp.sum(mask, axis=1, keepdims=True) - 1.0
    lane = lanes((TOK, 128))
    freq = jnp.exp((lane & 31).astype(F32) * (-2.0 * math.log(ROPE_BASE) / HS))
    angle = pos * freq
    cos_ref[...] = jnp.cos(angle)
    sine = jnp.sin(angle)
    sin_ref[...] = jnp.where((lane & 63) < 32, -sine, sine)

    def onward(p):
        for q in xpeers:
            piece = w_ref.at[q, p, c]
            remote(piece, piece, xsend, xrecv.at[q, p], sib).wait_recv()
        row = w_ref.at[:, p, c]
        remote(row, row, csend, crecv, sib).start()

    for n, p in enumerate(ypeers):
        piece = w_ref.at[x, p, c]
        remote(piece, piece, ysend, yrecv.at[p], sib).wait_recv()
        for q in xpeers:
            remote(piece, piece, xsend, xrecv.at[x, p], device(q, z, y, c)).start()
        if n >= 2:
            onward(ypeers[n - 2])
    onward(ypeers[5])
    onward(ypeers[6])
    half = w_ref.at[:, pl.ds(0, 4)]
    remote(half, half, csend, crecv, sib).wait()
    seven = w_ref.at[0, pl.ds(0, 7), 0]
    remote(seven, seven, ysend, yrecv.at[0], sib).wait_send()
    more = w_ref.at[pl.ds(0, 3), pl.ds(0, 7), 0]
    remote(more, more, xsend, yrecv.at[0], sib).wait_send()


def main_kernel(
    w_ref, hid_hbm, gm_hbm, nb_ref, irms_ref, cos_ref, sin_ref, mask_ref,
    mixed_ref, gh_ref, gout_ref,
    hid_ref, gm_ref, pin, pout, cin, cout, xin, xout, xrin, xrout, yout, yrout, ybuf, yrbuf, msg, rbuf,
    cs, cr, xs, xr, ys, yr, fs, fr, ls,
):
    x, z, y, c = coords()
    me = 2 * y + c
    sib = device(x, z, y, 1 - c)
    xpeers = [lax.rem(x + k, NX) for k in range(1, NX)]
    ypeers = [lax.rem(y + k, NY) for k in range(1, NY)]
    owner = 8 * c + y
    diagonal = z == owner
    barrier = pltpu.get_barrier_semaphore()
    signal(barrier, sib)
    for p in xpeers:
        signal(barrier, device(p, z, y, c))
    for p in ypeers:
        signal(barrier, device(x, z, p, c))
    sy, sc = lax.rem(z, 8), lax.div(z, 8)
    for k in range(1, NZ):
        signal(barrier, device(x, lax.rem(z + k, NZ), sy, sc))

    @pl.when(jnp.logical_not(diagonal))
    def _():
        signal(barrier, device(x, z, sy, sc))

    gm_load = pltpu.make_async_copy(gm_hbm, gm_ref, ls.at[0])
    gm_load.start()
    hid_load = pltpu.make_async_copy(hid_hbm, hid_ref, ls.at[1])
    hid_load.start()

    lo = lanes((TOK, 128)) < 64
    cos, sin = cos_ref[...], sin_ref[...]
    grad_scale = 131072 ** (-0.5)
    zero = jnp.zeros((TOK, 128), F32)

    nb = nb_ref[...]
    proj = [jnp.dot(nb, w_ref[t], preferred_element_type=F32) for t in range(2)]
    proj.append(jnp.dot(nb, w_ref[2, :, :128], preferred_element_type=F32))
    q = []
    for t in range(4):
        v = proj[t // 2][:, 128 * (t % 2) : 128 * (t % 2) + 128]
        q.append(v * cos + swap_halves(v) * sin)
    k_hi = jnp.where(lo, zero, q[3])
    k_lo = pltpu.roll(k_hi, 64, 1)
    q[3] = jnp.where(lo, q[3], zero)
    qb = [v.astype(BF16) for v in q]
    kk = jnp.concatenate([k_lo.astype(BF16), k_hi.astype(BF16)], axis=0)
    v_lo = jnp.where(lo, proj[2], zero)
    v_hi = pltpu.roll(v_lo, 64, 1)
    vv = jnp.concatenate([v_lo.astype(BF16), v_hi.astype(BF16)], axis=0)
    allowed = mask_ref[...] > 0.5
    probs, pb = [], []
    for t in range(4):
        s2 = lax.dot_general(qb[t], kk if t < 3 else kk[:128], NT, preferred_element_type=F32)
        for h in range(2 if t < 3 else 1):
            s = jnp.where(allowed, s2[:, 128 * h : 128 * h + 128] * 0.125, -1e30)
            e = jnp.exp(s - jnp.max(s, axis=1, keepdims=True))
            p = e * (1.0 / jnp.sum(e, axis=1, keepdims=True))
            probs.append(p)
            pb.append(p.astype(BF16))
    att = [jnp.dot(pb[0], vv[128:], preferred_element_type=F32).astype(BF16)]
    for t in range(1, 4):
        pair = jnp.concatenate([pb[2 * t - 1], pb[2 * t]], axis=1)
        att.append(jnp.dot(pair, vv, preferred_element_type=F32).astype(BF16))
    a = jnp.concatenate(att, axis=1)
    gm_load.wait()
    gm = gm_ref[...]
    src, dst = lanes((512, 512), 0), lanes((512, 512))
    want = 64 + 112 * ((dst >> 3) & 3) + 56 * (dst >> 8) + 7 * ((dst >> 5) & 7) + (dst & 7)
    order = jnp.where((src == want) & ((dst & 7) < 7), 1.0, 0.0).astype(BF16)
    ordered = jnp.dot(a, order, preferred_element_type=F32).astype(BF16)
    part = lax.dot_general(ordered, gm, TN, preferred_element_type=F32)
    for h in range(2):
        for p in range(NY):
            r = 256 * h + 32 * p
            pout[h, p] = (part[r : r + 32] * grad_scale).astype(BF16)
    pl.semaphore_wait(barrier, 27 - diagonal.astype(jnp.int32))
    copies = []
    for k in range(NY):
        p = lax.rem(y + 1 + k, NY)
        cp = remote(pout.at[1 - c, p], cout.at[p], cs.at[k], cr.at[p], sib)
        cp.start()
        copies.append(cp)

    ga = [jnp.dot(gm, w_ref[t], preferred_element_type=F32) for t in (2, 3)]
    g = [ga[t // 2][:, 128 * (t % 2) : 128 * (t % 2) + 128] for t in range(4)]
    g[0] = jnp.where(lo, zero, g[0])
    gb = [v.astype(BF16) for v in g]
    gs = [None] * 7
    for t in range(4):
        g2 = lax.dot_general(gb[t], vv if t > 0 else vv[128:], NT, preferred_element_type=F32)
        prod = gb[t].astype(F32) * att[t].astype(F32)
        for h in range(2 if t > 0 else 1):
            head = 2 * t - 1 + h if t > 0 else 0
            if t == 0:
                delta = jnp.sum(prod, axis=1, keepdims=True)
            else:
                delta = jnp.sum(jnp.where(lo, prod, zero) if h == 0 else jnp.where(lo, zero, prod), axis=1, keepdims=True)
            gp = g2[:, 128 * h : 128 * h + 128]
            gs[head] = (probs[head] * (gp - delta) * 0.125).astype(BF16)
    zb = jnp.zeros((TOK, 128), BF16)
    q_rows = [jnp.where(lo, q[h // 2], zero).astype(BF16) if h % 2 == 0 else jnp.where(lo, zero, q[h // 2]).astype(BF16) for h in range(7)]
    g_rows = [gb[0]] + [
        (jnp.where(lo, g[(h + 1) // 2], zero) if h % 2 == 1 else jnp.where(lo, zero, g[h // 2])).astype(BF16) for h in range(1, 7)
    ]
    gk = lax.dot_general(jnp.concatenate(gs, axis=0), jnp.concatenate(q_rows, axis=0), TN, preferred_element_type=F32)
    gk = gk + pltpu.roll(gk, 64, 1)
    gv = lax.dot_general(jnp.concatenate(pb, axis=0), jnp.concatenate(g_rows, axis=0), TN, preferred_element_type=F32)
    gv = gv + pltpu.roll(gv, 64, 1)
    tiles = []
    for t in range(4):
        if t < 3:
            pair = jnp.concatenate([gs[2 * t], gs[2 * t + 1]], axis=1)
            v = jnp.dot(pair, kk, preferred_element_type=F32)
        else:
            v = jnp.dot(gs[6], kk[:128], preferred_element_type=F32)
            v = jnp.where(lo, v, gk)
        tiles.append((v * cos - swap_halves(v) * sin).astype(BF16))
    tiles.append(jnp.where(lo, gv, zero).astype(BF16))
    gpa = jnp.concatenate(tiles, axis=1)
    part = lax.dot_general(nb, gpa, TN, preferred_element_type=F32)
    for h in range(2):
        for p in range(NX):
            r = 224 * p + 112 * h
            pin[h, p] = (part[r : r + 112] * grad_scale).astype(BF16)
    for k in range(NX):
        p = lax.rem(x + 1 + k, NX)
        cp = remote(pin.at[1 - c, p], cin.at[p], cs.at[8 + k], cr.at[8 + p], sib)
        cp.start()
        copies.append(cp)

    sum_out = sum_in = None
    for k in range(NY):
        p = lax.rem(y + 1 + k, NY)
        remote(pout.at[c, p], cout.at[p], cs.at[0], cr.at[p], sib).wait_recv()
        s = pout[c, p].astype(F32) + cout[p].astype(F32)
        if k < NY - 1:
            yout[k] = s.astype(BF16)
            cp = remote(yout.at[k], yrout.at[y], ys.at[8 + k], yr.at[8 + y], device(x, z, p, c))
            cp.start()
            copies.append(cp)
        else:
            sum_out = s
    for k in range(NX):
        p = lax.rem(x + 1 + k, NX)
        remote(pin.at[c, p], cin.at[p], cs.at[0], cr.at[8 + p], sib).wait_recv()
        s = pin[c, p].astype(F32) + cin[p].astype(F32)
        if k < NX - 1:
            xin[k] = s.astype(BF16)
            cp = remote(xin.at[k], xrin.at[x], xs.at[k], xr.at[x], device(p, z, y, c))
            cp.start()
            copies.append(cp)
        else:
            sum_in = s

    hid_load.wait()
    hid = hid_ref[...].astype(F32)
    out = sum(lax.dot_general(a[:, 256 * t : 256 * t + 256], w_ref[2 + t], NT, preferred_element_type=F32) for t in range(2))
    mixed_ref[...] = (hid + out).astype(BF16)
    gn = sum(lax.dot_general(gpa[:, 256 * t : 256 * t + 256], w_ref[t], NT, preferred_element_type=F32) for t in range(2))
    gn = gn + lax.dot_general(gpa[:, 512:], w_ref[2, :, :128], NT, preferred_element_type=F32)
    irms = irms_ref[:, :1]
    normed = hid * irms
    mean = jnp.mean(gn * normed, axis=1, keepdims=True)
    gh_ref[...] = ((gn - normed * mean) * irms + gm.astype(F32)).astype(BF16)

    for p in xpeers:
        remote(xin.at[0], xrin.at[p], xs.at[0], xr.at[p], sib).wait_recv()
        sum_in = sum_in + xrin[p].astype(F32)
    row, col = lanes((128, 112), 0), lanes((128, 112))
    pick_in = ((row & 7) < 7) & (col == 7 * (row >> 3) + (row & 7))
    e_in = jnp.where(pick_in, 1.0, 0.0).astype(BF16)
    y_in = jnp.dot(e_in, sum_in.astype(BF16), preferred_element_type=F32)
    for p in range(NY):
        ybuf[p] = y_in[16 * p : 16 * p + 16].astype(BF16)
    for k, p in enumerate(ypeers):
        cp = remote(ybuf.at[p], yrbuf.at[y], ys.at[k], yr.at[y], device(x, z, p, c))
        cp.start()
        copies.append(cp)

    for p in ypeers:
        remote(yout.at[0], yrout.at[p], ys.at[0], yr.at[8 + p], sib).wait_recv()
        sum_out = sum_out + yrout[p].astype(F32)
    for p in range(NX):
        xout[p] = sum_out[8 * p : 8 * p + 8]
    for k, p in enumerate(xpeers):
        cp = remote(xout.at[p], xrout.at[x], xs.at[4 + k], xr.at[4 + x], device(p, z, y, c))
        cp.start()
        copies.append(cp)
    sum_out = xout[x]
    for p in xpeers:
        remote(xout.at[0], xrout.at[p], xs.at[0], xr.at[4 + p], sib).wait_recv()
        sum_out = sum_out + xrout[p]
    high = lanes((8, 512)) >= 64
    left = jnp.where(high, pltpu.roll(sum_out[:, :512], 64, 1), 0.0)
    right = jnp.where(high, sum_out[:, 384:], 0.0)
    halves = jnp.concatenate([left, right], axis=0).astype(BF16)
    row, col = lanes((16, 16), 0), lanes((16, 16))
    q7 = 7 * (row >> 3) + (row & 7)
    e_out = jnp.where(((row & 7) < 7) & (col == (q7 >> 1) + 8 * (q7 & 1)), 1.0, 0.0).astype(BF16)
    y_out = jnp.dot(e_out, halves, preferred_element_type=F32)

    total = ybuf[y].astype(F32)
    for p in ypeers:
        remote(ybuf.at[0], yrbuf.at[p], ys.at[0], yr.at[p], sib).wait_recv()
        total = total + yrbuf[p].astype(F32)
    total = jnp.concatenate([total[:, :512], total[:, 512:] + y_out[:, :128], y_out[:, 128:]], axis=1)

    before = pltpu.roll(total, 1, 0)
    lane = lanes((16, 1024))
    jrow = lanes((16, 1024), 0) & 7
    flat = jnp.zeros((16, 1024), F32)
    for k in range(8):
        here = jnp.where(lane < 504, pltpu.roll(total, 72 * k, 1), pltpu.roll(total, (56 * k - 72) % 1024, 1))
        past = jnp.where(lane < 504, pltpu.roll(before, (448 + 72 * k) % 1024, 1), pltpu.roll(before, (504 + 56 * k) % 1024, 1))
        old = (lane < 72 * k) | ((lane >= 504) & (lane < 504 + 56 * k))
        flat = jnp.where(jrow == k, jnp.where(old, past, here), flat)
    for t in range(8):
        msg[:, t, :] = flat[:, 128 * t : 128 * t + 128].astype(BF16)
    for k in range(1, 16):
        i = lax.rem(me + k, 16)
        cp = remote(msg.at[i], rbuf.at[z], fs.at[k], fr.at[z], device(x, owner, lax.div(i, 2), lax.rem(i, 2)))
        cp.start()
        copies.append(cp)
    mine = remote(msg.at[me], rbuf.at[z], fs.at[0], fr.at[z], device(x, owner, y, c))
    kept = pltpu.make_async_copy(msg.at[me], rbuf.at[z], ls.at[2])

    @pl.when(diagonal)
    def _():
        kept.start()
        kept.wait()

    @pl.when(jnp.logical_not(diagonal))
    def _():
        mine.start()
        mine.wait_send()
        remote(msg.at[0], rbuf.at[z], fs.at[0], fr.at[z], sib).wait_recv()

    for k in range(1, 16):
        s = lax.rem(z + k, 16)
        remote(msg.at[0], rbuf.at[s], fs.at[0], fr.at[s], sib).wait_recv()
    total = jnp.sum(rbuf[...].astype(F32), axis=0)
    for t in range(8):
        gout_ref[:, 128 * t : 128 * t + 128] = total[t : t + 1]
    for cp in copies:
        cp.wait_send()


def write_kernel(mixed_ref, gh_ref, grads_ref, mixed_out, gh_out, in_out, out_out, sem):
    copies = [pltpu.make_async_copy(mixed_ref, mixed_out, sem.at[0]), pltpu.make_async_copy(gh_ref, gh_out, sem.at[1])]
    for cp in copies:
        cp.start()
    flat = grads_ref[...]
    in_out[...] = flat[:, :504]
    out_out[...] = pltpu.roll(flat, 520, 1)[:, :392]
    for cp in copies:
        cp.wait()


def body(hidden_in, doc_ids, grad_mixed, in_codes, in_scales, out_codes, out_scales):
    vm = pl.BlockSpec(memory_space=VMEM)
    hbm = pl.BlockSpec(memory_space=pltpu.HBM)
    dma = pltpu.SemaphoreType.DMA
    sds = jax.ShapeDtypeStruct
    tokens = sds((TOK, D), BF16)
    square = sds((TOK, 128), F32)
    held = [pltpu.with_memory_space_constraint(v, pltpu.HBM) for v in (in_codes, out_codes.T, in_scales.T, out_scales, hidden_in, doc_ids)]
    grad_mixed = pltpu.with_memory_space_constraint(grad_mixed, pltpu.HBM)
    w, nb, irms, cos, sin, mask = pl.pallas_call(
        gather_kernel,
        out_shape=(sds((4, 8, 2, 56, 256), BF16), tokens, square, square, square, square),
        in_specs=[hbm] * 6,
        out_specs=(vm,) * 6,
        scratch_shapes=[
            VMEM((56, 576), BF16), VMEM((56, 448), BF16), VMEM((9, 28), F32), VMEM((7, 28), F32),
            VMEM((TOK, D), BF16), VMEM((1, 128), jnp.int32), VMEM((56, 128), F32),
            dma((6,)), dma, dma((8,)), dma, dma((4, 8)), dma, dma,
        ],
        compiler_params=pltpu.CompilerParams(collective_id=0, has_side_effects=True, vmem_limit_bytes=16 << 20),
        name="gather",
    )(*held)
    mixed, grad_hidden, grads = pl.pallas_call(
        main_kernel,
        out_shape=(tokens, tokens, sds((1, 1024), F32)),
        in_specs=[vm, hbm, hbm] + [vm] * 5,
        out_specs=(vm, vm, vm),
        scratch_shapes=[
            VMEM((TOK, D), BF16), VMEM((TOK, D), BF16),
            VMEM((2, 4, 112, 640), BF16), VMEM((2, 8, 32, 896), BF16),
            VMEM((4, 112, 640), BF16), VMEM((8, 32, 896), BF16),
            VMEM((3, 112, 640), BF16), VMEM((4, 8, 896), F32),
            VMEM((4, 112, 640), BF16), VMEM((4, 8, 896), F32),
            VMEM((7, 32, 896), BF16), VMEM((8, 32, 896), BF16),
            VMEM((8, 16, 640), BF16), VMEM((8, 16, 640), BF16),
            VMEM((16, 8, 128), BF16), VMEM((16, 8, 128), BF16),
            dma((12,)), dma((12,)), dma((8,)), dma((8,)), dma((15,)), dma((16,)), dma((16,)), dma((16,)), dma((3,)),
        ],
        compiler_params=pltpu.CompilerParams(collective_id=1, has_side_effects=True, vmem_limit_bytes=32 << 20),
        name="sublayer",
    )(w.reshape(4, D, 256), held[4], grad_mixed, nb, irms, cos, sin, mask)
    mixed, grad_hidden, grad_in, grad_out = pl.pallas_call(
        write_kernel,
        out_shape=(pltpu.HBM((TOK, D), BF16), pltpu.HBM((TOK, D), BF16), pltpu.HBM((1, 504), F32), pltpu.HBM((1, 392), F32)),
        in_specs=[vm] * 3,
        out_specs=(hbm, hbm, pl.BlockSpec(), pl.BlockSpec()),
        scratch_shapes=[dma((2,))],
        name="write",
    )(*(pltpu.with_memory_space_constraint(v, VMEM) for v in (mixed, grad_hidden, grads)))
    return mixed, grad_hidden, grad_in.reshape(504), grad_out.reshape(392)


def solution(mesh):
    rows = P(("outer", "inner"), None)
    return jax.shard_map(
        body,
        mesh=mesh,
        in_specs=(rows, rows, rows, P("inner", None), P(), P(None, "inner"), P()),
        out_specs=(rows, rows, P(("outer", "inner")), P(("outer", "inner"))),
        check_vma=False,
    )
```

```python
import math

import jax
import jax.numpy as jnp
from jax import lax
from jax.experimental import pallas as pl
from jax.experimental.pallas import tpu as pltpu
from jax.sharding import PartitionSpec as P

MESH = pl.DeviceIdType.MESH
F32, BF16 = jnp.float32, jnp.bfloat16
D, HEADS, HS = 896, 7, 64
TOK = 128
NX, NZ, NY = 4, 16, 8
NEAR = 2
ROPE_BASE = 1000000.0
EPS = 1e-06
VMEM = pltpu.VMEM
NT = (((1,), (1,)), ((), ()))
TN = (((0,), (0,)), ((), ()))


def coords():
    o = lax.axis_index("outer")
    i = lax.axis_index("inner")
    return lax.div(o, 16), lax.rem(o, 16), lax.div(i, 2), lax.rem(i, 2)


def device(x, z, y, c):
    return (x * 16 + z, y * 2 + c)


def signal(sem, dev):
    pl.semaphore_signal(sem, inc=1, device_id=dev, device_id_type=MESH)


def remote(src, dst, send, recv, dev):
    return pltpu.make_async_remote_copy(
        src_ref=src, dst_ref=dst, send_sem=send, recv_sem=recv, device_id=dev, device_id_type=MESH
    )


def lanes(shape, dim=1):
    return lax.broadcasted_iota(jnp.int32, shape, dim)


def swap_halves(v):
    low = (lanes(v.shape) & 63) < 32
    return jnp.where(low, pltpu.roll(v, 96, 1), pltpu.roll(v, 32, 1))


def allowed_pairs(doc_ref):
    row = jnp.broadcast_to(doc_ref[...].astype(F32), (TOK, TOK))
    return (row == row.T) & (lanes((TOK, TOK)) <= lanes((TOK, TOK), 0))


def gather_kernel(
    inc_ref, outc_ref, ins_ref, outs_ref, hid_ref, doc_ref,
    w_ref, nb_ref, irms_ref, cos_ref, sin_ref, mask_ref,
    ic, oc, ins, outs, hid, doc, pad, lsem, ysend, nsend, yrecv, xsend, xrecv, csend, crecv,
):
    x, z, y, c = coords()
    me = 2 * y + c
    sib = device(x, z, y, 1 - c)
    xpeers = [lax.rem(x + k, NX) for k in (1, 3, 2)]
    ypeers = [lax.rem(y + k, NY) for k in (1, 7, 2, 6, 3, 5, 4)]
    near, far = ypeers[:NEAR], ypeers[NEAR:]
    barrier = pltpu.get_barrier_semaphore()
    for p in ypeers:
        signal(barrier, device(x, z, p, c))
    for p in xpeers:
        signal(barrier, device(p, z, y, c))
    signal(barrier, sib)
    pairs = ((inc_ref, ic), (outc_ref, oc), (ins_ref, ins), (outs_ref, outs), (doc_ref, doc), (hid_ref, hid))
    loads = [pltpu.make_async_copy(src, dst, lsem.at[k]) for k, (src, dst) in enumerate(pairs)]
    for cp in loads:
        cp.start()
    pad[...] = jnp.zeros((56, 128), F32)
    for cp in loads[:4]:
        cp.wait()

    shift = jnp.where(lanes((448, 512)) == lanes((448, 512), 0) + 64, 1.0, 0.0).astype(BF16)
    turned = jnp.dot(oc[...], shift, preferred_element_type=F32)
    block = (lanes((56, 28), 0) + 56 * me) >> 5
    pick = jnp.where(block == lanes((56, 28)), 1.0, 0.0)
    s_in = lax.dot_general(pick, ins[...], NT, precision=lax.Precision.HIGHEST, preferred_element_type=F32)
    s_out = lax.dot_general(pick, outs[...], NT, precision=lax.Precision.HIGHEST, preferred_element_type=F32)
    columns = [s_in[:, k : k + 1] for k in range(9)] + [s_out[:, k : k + 1] for k in range(7)]
    low = lanes((56, 128)) < 64
    pad[:, :64] = ic[:, 512:].astype(F32)
    for t in range(8):
        if t < 4:
            code = ic[:, 128 * t : 128 * t + 128].astype(F32)
        else:
            code = turned[:, 128 * t - 512 : 128 * t - 384]
            if t == 4:
                code = code + pad[...]
        scale = jnp.where(low, columns[2 * t], columns[2 * t + 1])
        w_ref[t // 2, y, c, :, 128 * (t % 2) : 128 * (t % 2) + 128] = (code * scale).astype(BF16)

    pl.semaphore_wait(barrier, 11)
    mine = w_ref.at[x, y, c]
    whole = w_ref.at[:, y, c]
    for p in far:
        remote(mine, mine, ysend, yrecv.at[y], device(x, z, p, c)).start()
    for p in near:
        remote(whole, whole, nsend, yrecv.at[y], device(x, z, p, c)).start()
    remote(whole, whole, csend, crecv, sib).start()

    loads[4].wait()
    loads[5].wait()
    rows = hid[...].astype(F32)
    irms = lax.rsqrt(jnp.mean(rows * rows, axis=1, keepdims=True) + EPS)
    nb_ref[...] = (rows * irms).astype(BF16)
    irms_ref[...] = jnp.broadcast_to(irms, (TOK, 128))
    mask = jnp.where(allowed_pairs(doc), 1.0, 0.0)
    mask_ref[...] = mask
    pos = jnp.sum(mask, axis=1, keepdims=True) - 1.0
    lane = lanes((TOK, 128))
    freq = jnp.exp((lane & 31).astype(F32) * (-2.0 * math.log(ROPE_BASE) / HS))
    angle = pos * freq
    cos_ref[...] = jnp.cos(angle)
    sine = jnp.sin(angle)
    sin_ref[...] = jnp.where((lane & 63) < 32, -sine, sine)

    def share(p):
        row = w_ref.at[:, p, c]
        remote(row, row, csend, crecv, sib).start()

    def onward(p):
        for q in xpeers:
            piece = w_ref.at[q, p, c]
            remote(piece, piece, xsend, xrecv.at[q, p], sib).wait_recv()
        share(p)

    for p in far:
        piece = w_ref.at[x, p, c]
        remote(piece, piece, ysend, yrecv.at[p], sib).wait_recv()
        for q in xpeers:
            remote(piece, piece, xsend, xrecv.at[x, p], device(q, z, y, c)).start()
    for n, p in enumerate(far):
        onward(p)
        if n < NEAR:
            row = w_ref.at[:, near[n], c]
            remote(row, row, ysend, yrecv.at[near[n]], sib).wait_recv()
            share(near[n])
    half = w_ref.at[:, pl.ds(0, 4)]
    remote(half, half, csend, crecv, sib).wait()
    sent = w_ref.at[0, pl.ds(0, 7 - NEAR), 0]
    remote(sent, sent, ysend, yrecv.at[0], sib).wait_send()
    sent = w_ref.at[:, pl.ds(0, NEAR), 0]
    remote(sent, sent, nsend, yrecv.at[0], sib).wait_send()
    sent = w_ref.at[pl.ds(0, 3), pl.ds(0, 7 - NEAR), 0]
    remote(sent, sent, xsend, yrecv.at[0], sib).wait_send()


def main_kernel(
    w_ref, hid_hbm, gm_hbm, nb_ref, irms_ref, cos_ref, sin_ref, mask_ref,
    mixed_ref, gh_ref, gout_ref,
    hid_ref, gm_ref, pin, pout, cin, cout, xin, xout, xrin, xrout, yout, yrout, ybuf, yrbuf, msg, rbuf,
    cs, cr, xs, xr, ys, yr, fs, fr, ls,
):
    x, z, y, c = coords()
    me = 2 * y + c
    sib = device(x, z, y, 1 - c)
    xpeers = [lax.rem(x + k, NX) for k in range(1, NX)]
    ypeers = [lax.rem(y + k, NY) for k in range(1, NY)]
    group, quad = lax.div(y, 4), lax.rem(y, 4)
    sy, sc = 4 * group + lax.div(lax.rem(z, 8), 2), lax.div(z, 8)
    diagonal = jnp.logical_and(sy == y, sc == c)
    barrier = pltpu.get_barrier_semaphore()
    signal(barrier, sib)
    for p in xpeers:
        signal(barrier, device(p, z, y, c))
    for p in ypeers:
        signal(barrier, device(x, z, p, c))
    for k in range(1, NZ):
        signal(barrier, device(x, lax.rem(z + k, NZ), sy, sc))

    @pl.when(jnp.logical_not(diagonal))
    def _():
        signal(barrier, device(x, z, sy, sc))

    gm_load = pltpu.make_async_copy(gm_hbm, gm_ref, ls.at[0])
    gm_load.start()
    hid_load = pltpu.make_async_copy(hid_hbm, hid_ref, ls.at[1])
    hid_load.start()

    lo = lanes((TOK, 128)) < 64
    cos, sin = cos_ref[...], sin_ref[...]
    grad_scale = 131072 ** (-0.5)
    zero = jnp.zeros((TOK, 128), F32)

    nb = nb_ref[...]
    proj = [jnp.dot(nb, w_ref[t], preferred_element_type=F32) for t in range(2)]
    proj.append(jnp.dot(nb, w_ref[2, :, :128], preferred_element_type=F32))
    q = []
    for t in range(4):
        v = proj[t // 2][:, 128 * (t % 2) : 128 * (t % 2) + 128]
        q.append(v * cos + swap_halves(v) * sin)
    k_hi = jnp.where(lo, zero, q[3])
    k_lo = pltpu.roll(k_hi, 64, 1)
    q[3] = jnp.where(lo, q[3], zero)
    qb = [v.astype(BF16) for v in q]
    kk = jnp.concatenate([k_lo.astype(BF16), k_hi.astype(BF16)], axis=0)
    v_lo = jnp.where(lo, proj[2], zero)
    v_hi = pltpu.roll(v_lo, 64, 1)
    vv = jnp.concatenate([v_lo.astype(BF16), v_hi.astype(BF16)], axis=0)
    allowed = mask_ref[...] > 0.5
    probs, pb = [], []
    for t in range(4):
        s2 = lax.dot_general(qb[t], kk if t < 3 else kk[:128], NT, preferred_element_type=F32)
        for h in range(2 if t < 3 else 1):
            s = jnp.where(allowed, s2[:, 128 * h : 128 * h + 128] * 0.125, -1e30)
            e = jnp.exp(s - jnp.max(s, axis=1, keepdims=True))
            p = e * (1.0 / jnp.sum(e, axis=1, keepdims=True))
            probs.append(p)
            pb.append(p.astype(BF16))
    att = [jnp.dot(pb[0], vv[128:], preferred_element_type=F32).astype(BF16)]
    for t in range(1, 4):
        pair = jnp.concatenate([pb[2 * t - 1], pb[2 * t]], axis=1)
        att.append(jnp.dot(pair, vv, preferred_element_type=F32).astype(BF16))
    a = jnp.concatenate(att, axis=1)
    gm_load.wait()
    gm = gm_ref[...]
    src, dst = lanes((512, 512), 0), lanes((512, 512))
    block = 7 * (2 * ((dst >> 5) & 3) + ((dst >> 2) & 1)) + 3 * ((dst >> 7) & 1) + (dst & 3)
    want = 64 + 112 * ((dst >> 3) & 3) + 56 * (dst >> 8) + block
    order = jnp.where(src == want, 1.0, 0.0).astype(BF16)
    ordered = jnp.dot(a, order, preferred_element_type=F32).astype(BF16)
    part = lax.dot_general(ordered, gm, TN, preferred_element_type=F32)
    for h in range(2):
        for p in range(NY):
            r = 256 * h + 32 * p
            pout[h, p] = (part[r : r + 32] * grad_scale).astype(BF16)
    pl.semaphore_wait(barrier, 27 - diagonal.astype(jnp.int32))
    copies = []
    for k in range(NY):
        p = lax.rem(y + 1 + k, NY)
        cp = remote(pout.at[1 - c, p], cout.at[p], cs.at[k], cr.at[p], sib)
        cp.start()
        copies.append(cp)

    ga = [jnp.dot(gm, w_ref[t], preferred_element_type=F32) for t in (2, 3)]
    g = [ga[t // 2][:, 128 * (t % 2) : 128 * (t % 2) + 128] for t in range(4)]
    g[0] = jnp.where(lo, zero, g[0])
    gb = [v.astype(BF16) for v in g]
    gs = [None] * 7
    for t in range(4):
        g2 = lax.dot_general(gb[t], vv if t > 0 else vv[128:], NT, preferred_element_type=F32)
        prod = gb[t].astype(F32) * att[t].astype(F32)
        for h in range(2 if t > 0 else 1):
            head = 2 * t - 1 + h if t > 0 else 0
            if t == 0:
                delta = jnp.sum(prod, axis=1, keepdims=True)
            else:
                delta = jnp.sum(jnp.where(lo, prod, zero) if h == 0 else jnp.where(lo, zero, prod), axis=1, keepdims=True)
            gp = g2[:, 128 * h : 128 * h + 128]
            gs[head] = (probs[head] * (gp - delta) * 0.125).astype(BF16)
    zb = jnp.zeros((TOK, 128), BF16)
    q_rows = [jnp.where(lo, q[h // 2], zero).astype(BF16) if h % 2 == 0 else jnp.where(lo, zero, q[h // 2]).astype(BF16) for h in range(7)]
    g_rows = [gb[0]] + [
        (jnp.where(lo, g[(h + 1) // 2], zero) if h % 2 == 1 else jnp.where(lo, zero, g[h // 2])).astype(BF16) for h in range(1, 7)
    ]
    gk = lax.dot_general(jnp.concatenate(gs, axis=0), jnp.concatenate(q_rows, axis=0), TN, preferred_element_type=F32)
    gk = gk + pltpu.roll(gk, 64, 1)
    gv = lax.dot_general(jnp.concatenate(pb, axis=0), jnp.concatenate(g_rows, axis=0), TN, preferred_element_type=F32)
    gv = gv + pltpu.roll(gv, 64, 1)
    tiles = []
    for t in range(4):
        if t < 3:
            pair = jnp.concatenate([gs[2 * t], gs[2 * t + 1]], axis=1)
            v = jnp.dot(pair, kk, preferred_element_type=F32)
        else:
            v = jnp.dot(gs[6], kk[:128], preferred_element_type=F32)
            v = jnp.where(lo, v, gk)
        tiles.append((v * cos - swap_halves(v) * sin).astype(BF16))
    tiles.append(jnp.where(lo, gv, zero).astype(BF16))
    gpa = jnp.concatenate(tiles, axis=1)
    part = lax.dot_general(nb, gpa, TN, preferred_element_type=F32)
    for h in range(2):
        for p in range(NX):
            r = 224 * p + 112 * h
            pin[h, p] = (part[r : r + 112] * grad_scale).astype(BF16)
    for k in range(NX):
        p = lax.rem(x + 1 + k, NX)
        cp = remote(pin.at[1 - c, p], cin.at[p], cs.at[8 + k], cr.at[8 + p], sib)
        cp.start()
        copies.append(cp)

    sum_out = sum_in = None
    for k in range(NY):
        p = lax.rem(y + 1 + k, NY)
        remote(pout.at[c, p], cout.at[p], cs.at[0], cr.at[p], sib).wait_recv()
        s = pout[c, p].astype(F32) + cout[p].astype(F32)
        if k < NY - 1:
            yout[k] = s.astype(BF16)
            cp = remote(yout.at[k], yrout.at[y], ys.at[8 + k], yr.at[8 + y], device(x, z, p, c))
            cp.start()
            copies.append(cp)
        else:
            sum_out = s
    for k in range(NX):
        p = lax.rem(x + 1 + k, NX)
        remote(pin.at[c, p], cin.at[p], cs.at[0], cr.at[8 + p], sib).wait_recv()
        s = pin[c, p].astype(F32) + cin[p].astype(F32)
        if k < NX - 1:
            xin[k] = s.astype(BF16)
            cp = remote(xin.at[k], xrin.at[x], xs.at[k], xr.at[x], device(p, z, y, c))
            cp.start()
            copies.append(cp)
        else:
            sum_in = s

    hid_load.wait()
    hid = hid_ref[...].astype(F32)
    out = sum(lax.dot_general(a[:, 256 * t : 256 * t + 256], w_ref[2 + t], NT, preferred_element_type=F32) for t in range(2))
    mixed_ref[...] = (hid + out).astype(BF16)
    gn = sum(lax.dot_general(gpa[:, 256 * t : 256 * t + 256], w_ref[t], NT, preferred_element_type=F32) for t in range(2))
    gn = gn + lax.dot_general(gpa[:, 512:], w_ref[2, :, :128], NT, preferred_element_type=F32)
    irms = irms_ref[:, :1]
    normed = hid * irms
    mean = jnp.mean(gn * normed, axis=1, keepdims=True)
    gh_ref[...] = ((gn - normed * mean) * irms + gm.astype(F32)).astype(BF16)

    row, col = lanes((128, 112), 0), lanes((128, 112))
    from_row = 14 * (2 * ((row >> 4) & 3) + ((row >> 3) & 1)) + 7 * (row >> 6) + (row & 7)
    e_in = jnp.where(((row & 7) < 7) & (col == from_row), 1.0, 0.0).astype(BF16)
    row, col = lanes((16, 16), 0), lanes((16, 16))
    turn = (row & 7) + group
    e_out = jnp.where(((row & 7) < 7) & (col == 4 * (row >> 3) + (turn >> 1) + 8 * (turn & 1)), 1.0, 0.0).astype(BF16)
    for p in xpeers:
        remote(xin.at[0], xrin.at[p], xs.at[0], xr.at[p], sib).wait_recv()
        sum_in = sum_in + xrin[p].astype(F32)
    y_in = jnp.dot(e_in, sum_in.astype(BF16), preferred_element_type=F32)
    for p in range(NY):
        ybuf[p] = y_in[16 * p : 16 * p + 16].astype(BF16)
    for k, p in enumerate(ypeers):
        cp = remote(ybuf.at[p], yrbuf.at[y], ys.at[k], yr.at[y], device(x, z, p, c))
        cp.start()
        copies.append(cp)

    for p in ypeers:
        remote(yout.at[0], yrout.at[p], ys.at[0], yr.at[8 + p], sib).wait_recv()
        sum_out = sum_out + yrout[p].astype(F32)
    for p in range(NX):
        xout[p] = sum_out[8 * p : 8 * p + 8]
    for k, p in enumerate(xpeers):
        cp = remote(xout.at[p], xrout.at[x], xs.at[4 + k], xr.at[4 + x], device(p, z, y, c))
        cp.start()
        copies.append(cp)
    sum_out = xout[x]
    for p in xpeers:
        remote(xout.at[0], xrout.at[p], xs.at[0], xr.at[4 + p], sib).wait_recv()
        sum_out = sum_out + xrout[p]
    left, right = sum_out[:, :512], pltpu.roll(sum_out[:, 384:], 448, 1)
    halves = jnp.concatenate([left, right], axis=0).astype(BF16)
    y_out = jnp.dot(e_out, halves, preferred_element_type=F32)
    before = pltpu.roll(y_out, 1, 0)
    lane, jrow = lanes((16, 512)), lanes((16, 512), 0) & 7
    flat_out = jnp.zeros((16, 512), F32)
    for k in range(8):
        old = lane < 56 * k + 120
        here, past = pltpu.roll(y_out, (120 + 56 * k) % 512, 1), pltpu.roll(before, (184 + 56 * k) % 512, 1)
        flat_out = jnp.where(jrow == k, jnp.where(old, past, here), flat_out)

    total = ybuf[y].astype(F32)
    for p in ypeers:
        remote(ybuf.at[0], yrbuf.at[p], ys.at[0], yr.at[p], sib).wait_recv()
        total = total + yrbuf[p].astype(F32)

    before = pltpu.roll(total, 1, 0)
    lane, jrow = lanes((16, 640)), lanes((16, 640), 0) & 7
    flat_in = jnp.zeros((16, 640), F32)
    for k in range(8):
        here, past = pltpu.roll(total, 72 * k, 1), pltpu.roll(before, 64 + 72 * k, 1)
        flat_in = jnp.where(jrow == k, jnp.where(lane < 72 * k, past, here), flat_in)
    seam = jnp.where(lanes((16, 128)) < 120, flat_in[:, 384:512], flat_out[:, :128])
    flat = jnp.concatenate([flat_in[:, :384], seam, flat_out[:, 128:], jnp.zeros((16, 128), F32)], axis=1)
    for t in range(8):
        msg[:, t, :] = flat[:, 128 * t : 128 * t + 128].astype(BF16)
    own = 8 * lax.rem(z, 2) + lax.rem(me, 8)

    def target(i):
        n = lax.rem(i, 8)
        return device(x, 8 * c + 2 * quad + lax.div(i, 8), 4 * group + lax.div(n, 2), lax.rem(n, 2))

    for k in range(1, 16):
        i = lax.rem(own + k, 16)
        cp = remote(msg.at[i], rbuf.at[z], fs.at[k], fr.at[z], target(i))
        cp.start()
        copies.append(cp)
    mine = remote(msg.at[own], rbuf.at[z], fs.at[0], fr.at[z], target(own))
    kept = pltpu.make_async_copy(msg.at[own], rbuf.at[z], ls.at[2])

    @pl.when(diagonal)
    def _():
        kept.start()
        kept.wait()

    @pl.when(jnp.logical_not(diagonal))
    def _():
        mine.start()
        mine.wait_send()
        remote(msg.at[0], rbuf.at[z], fs.at[0], fr.at[z], sib).wait_recv()

    for k in range(1, 16):
        s = lax.rem(z + k, 16)
        remote(msg.at[0], rbuf.at[s], fs.at[0], fr.at[s], sib).wait_recv()
    total = jnp.sum(rbuf[...].astype(F32), axis=0)
    for t in range(8):
        gout_ref[:, 128 * t : 128 * t + 128] = total[t : t + 1]
    for cp in copies:
        cp.wait_send()


def write_kernel(mixed_ref, gh_ref, grads_ref, mixed_out, gh_out, in_out, out_out, sem):
    copies = [pltpu.make_async_copy(mixed_ref, mixed_out, sem.at[0]), pltpu.make_async_copy(gh_ref, gh_out, sem.at[1])]
    for cp in copies:
        cp.start()
    flat = grads_ref[...]
    in_out[...] = flat[:, :504]
    out_out[...] = pltpu.roll(flat, 520, 1)[:, :392]
    for cp in copies:
        cp.wait()


def body(hidden_in, doc_ids, grad_mixed, in_codes, in_scales, out_codes, out_scales):
    vm = pl.BlockSpec(memory_space=VMEM)
    hbm = pl.BlockSpec(memory_space=pltpu.HBM)
    dma = pltpu.SemaphoreType.DMA
    sds = jax.ShapeDtypeStruct
    tokens = sds((TOK, D), BF16)
    square = sds((TOK, 128), F32)
    held = [pltpu.with_memory_space_constraint(v, pltpu.HBM) for v in (in_codes, out_codes.T, in_scales.T, out_scales, hidden_in, doc_ids)]
    grad_mixed = pltpu.with_memory_space_constraint(grad_mixed, pltpu.HBM)
    w, nb, irms, cos, sin, mask = pl.pallas_call(
        gather_kernel,
        out_shape=(sds((4, 8, 2, 56, 256), BF16), tokens, square, square, square, square),
        in_specs=[hbm] * 6,
        out_specs=(vm,) * 6,
        scratch_shapes=[
            VMEM((56, 576), BF16), VMEM((56, 448), BF16), VMEM((9, 28), F32), VMEM((7, 28), F32),
            VMEM((TOK, D), BF16), VMEM((1, 128), jnp.int32), VMEM((56, 128), F32),
            dma((6,)), dma, dma, dma((8,)), dma, dma((4, 8)), dma, dma,
        ],
        compiler_params=pltpu.CompilerParams(collective_id=0, has_side_effects=True, vmem_limit_bytes=16 << 20),
        name="gather",
    )(*held)
    mixed, grad_hidden, grads = pl.pallas_call(
        main_kernel,
        out_shape=(tokens, tokens, sds((1, 1024), F32)),
        in_specs=[vm, hbm, hbm] + [vm] * 5,
        out_specs=(vm, vm, vm),
        scratch_shapes=[
            VMEM((TOK, D), BF16), VMEM((TOK, D), BF16),
            VMEM((2, 4, 112, 640), BF16), VMEM((2, 8, 32, 896), BF16),
            VMEM((4, 112, 640), BF16), VMEM((8, 32, 896), BF16),
            VMEM((3, 112, 640), BF16), VMEM((4, 8, 896), F32),
            VMEM((4, 112, 640), BF16), VMEM((4, 8, 896), F32),
            VMEM((7, 32, 896), BF16), VMEM((8, 32, 896), BF16),
            VMEM((8, 16, 640), BF16), VMEM((8, 16, 640), BF16),
            VMEM((16, 8, 128), BF16), VMEM((16, 8, 128), BF16),
            dma((12,)), dma((12,)), dma((8,)), dma((8,)), dma((15,)), dma((16,)), dma((16,)), dma((16,)), dma((3,)),
        ],
        compiler_params=pltpu.CompilerParams(collective_id=1, has_side_effects=True, vmem_limit_bytes=32 << 20),
        name="sublayer",
    )(w.reshape(4, D, 256), held[4], grad_mixed, nb, irms, cos, sin, mask)
    mixed, grad_hidden, grad_in, grad_out = pl.pallas_call(
        write_kernel,
        out_shape=(pltpu.HBM((TOK, D), BF16), pltpu.HBM((TOK, D), BF16), pltpu.HBM((1, 504), F32), pltpu.HBM((1, 392), F32)),
        in_specs=[vm] * 3,
        out_specs=(hbm, hbm, pl.BlockSpec(), pl.BlockSpec()),
        scratch_shapes=[dma((2,))],
        name="write",
    )(*(pltpu.with_memory_space_constraint(v, VMEM) for v in (mixed, grad_hidden, grads)))
    return mixed, grad_hidden, grad_in.reshape(504), grad_out.reshape(392)


def solution(mesh):
    rows = P(("outer", "inner"), None)
    return jax.shard_map(
        body,
        mesh=mesh,
        in_specs=(rows, rows, rows, P("inner", None), P(), P(None, "inner"), P()),
        out_specs=(rows, rows, P(("outer", "inner")), P(("outer", "inner"))),
        check_vma=False,
    )
```

```python
import math

import jax
import jax.numpy as jnp
from jax import lax
from jax.experimental import pallas as pl
from jax.experimental.pallas import tpu as pltpu
from jax.sharding import PartitionSpec as P

MESH = pl.DeviceIdType.MESH
F32, BF16 = jnp.float32, jnp.bfloat16
D, HEADS, HS = 896, 7, 64
TOK = 128
NX, NZ, NY = 4, 16, 8
NEAR = 2
ROPE_BASE = 1000000.0
EPS = 1e-06
VMEM = pltpu.VMEM
NT = (((1,), (1,)), ((), ()))
TN = (((0,), (0,)), ((), ()))


def coords():
    o = lax.axis_index("outer")
    i = lax.axis_index("inner")
    return lax.div(o, 16), lax.rem(o, 16), lax.div(i, 2), lax.rem(i, 2)


def device(x, z, y, c):
    return (x * 16 + z, y * 2 + c)


def signal(sem, dev):
    pl.semaphore_signal(sem, inc=1, device_id=dev, device_id_type=MESH)


def remote(src, dst, send, recv, dev):
    return pltpu.make_async_remote_copy(
        src_ref=src, dst_ref=dst, send_sem=send, recv_sem=recv, device_id=dev, device_id_type=MESH
    )


def lanes(shape, dim=1):
    return lax.broadcasted_iota(jnp.int32, shape, dim)


def swap_halves(v):
    low = (lanes(v.shape) & 63) < 32
    return jnp.where(low, pltpu.roll(v, 96, 1), pltpu.roll(v, 32, 1))


def allowed_pairs(doc_ref):
    row = jnp.broadcast_to(doc_ref[...].astype(F32), (TOK, TOK))
    return (row == row.T) & (lanes((TOK, TOK)) <= lanes((TOK, TOK), 0))


def gather_kernel(
    inc_ref, outc_ref, ins_ref, outs_ref, hid_ref, doc_ref,
    w_ref, nb_ref, irms_ref, cos_ref, sin_ref, mask_ref,
    ic, oc, ins, outs, hid, doc, pad, lsem, ysend, nsend, yrecv, xsend, xrecv, csend, crecv,
):
    x, z, y, c = coords()
    me = 2 * y + c
    sib = device(x, z, y, 1 - c)
    xpeers = [lax.rem(x + k, NX) for k in (1, 3, 2)]
    ypeers = [lax.rem(y + k, NY) for k in (1, 7, 2, 6, 3, 5, 4)]
    near, far = ypeers[:NEAR], ypeers[NEAR:]
    barrier = pltpu.get_barrier_semaphore()
    for p in ypeers:
        signal(barrier, device(x, z, p, c))
    for p in xpeers:
        signal(barrier, device(p, z, y, c))
    signal(barrier, sib)
    pairs = ((inc_ref, ic), (outc_ref, oc), (ins_ref, ins), (outs_ref, outs), (doc_ref, doc), (hid_ref, hid))
    loads = [pltpu.make_async_copy(src, dst, lsem.at[k]) for k, (src, dst) in enumerate(pairs)]
    for cp in loads:
        cp.start()
    pad[...] = jnp.zeros((56, 128), F32)
    for cp in loads[:4]:
        cp.wait()

    shift = jnp.where(lanes((448, 512)) == lanes((448, 512), 0) + 64, 1.0, 0.0).astype(BF16)
    turned = jnp.dot(oc[...], shift, preferred_element_type=F32)
    block = (lanes((56, 28), 0) + 56 * me) >> 5
    pick = jnp.where(block == lanes((56, 28)), 1.0, 0.0)
    s_in = lax.dot_general(pick, ins[...], NT, precision=lax.Precision.HIGHEST, preferred_element_type=F32)
    s_out = lax.dot_general(pick, outs[...], NT, precision=lax.Precision.HIGHEST, preferred_element_type=F32)
    columns = [s_in[:, k : k + 1] for k in range(9)] + [s_out[:, k : k + 1] for k in range(7)]
    low = lanes((56, 128)) < 64
    pad[:, :64] = ic[:, 512:].astype(F32)
    for t in range(8):
        if t < 4:
            code = ic[:, 128 * t : 128 * t + 128].astype(F32)
        else:
            code = turned[:, 128 * t - 512 : 128 * t - 384]
            if t == 4:
                code = code + pad[...]
        scale = jnp.where(low, columns[2 * t], columns[2 * t + 1])
        w_ref[t // 2, y, c, :, 128 * (t % 2) : 128 * (t % 2) + 128] = (code * scale).astype(BF16)

    pl.semaphore_wait(barrier, 11)
    mine = w_ref.at[x, y, c]
    whole = w_ref.at[:, y, c]
    for p in far:
        remote(mine, mine, ysend, yrecv.at[y], device(x, z, p, c)).start()
    for p in near:
        remote(whole, whole, nsend, yrecv.at[y], device(x, z, p, c)).start()
    remote(whole, whole, csend, crecv, sib).start()

    loads[4].wait()
    loads[5].wait()
    rows = hid[...].astype(F32)
    irms = lax.rsqrt(jnp.mean(rows * rows, axis=1, keepdims=True) + EPS)
    nb_ref[...] = (rows * irms).astype(BF16)
    irms_ref[...] = jnp.broadcast_to(irms, (TOK, 128))
    mask = jnp.where(allowed_pairs(doc), 1.0, 0.0)
    mask_ref[...] = mask
    pos = jnp.sum(mask, axis=1, keepdims=True) - 1.0
    lane = lanes((TOK, 128))
    freq = jnp.exp((lane & 31).astype(F32) * (-2.0 * math.log(ROPE_BASE) / HS))
    angle = pos * freq
    cos_ref[...] = jnp.cos(angle)
    sine = jnp.sin(angle)
    sin_ref[...] = jnp.where((lane & 63) < 32, -sine, sine)

    def share(p):
        row = w_ref.at[:, p, c]
        remote(row, row, csend, crecv, sib).start()

    def onward(p):
        for q in xpeers:
            piece = w_ref.at[q, p, c]
            remote(piece, piece, xsend, xrecv.at[q, p], sib).wait_recv()
        share(p)

    for p in far:
        piece = w_ref.at[x, p, c]
        remote(piece, piece, ysend, yrecv.at[p], sib).wait_recv()
        for q in xpeers:
            remote(piece, piece, xsend, xrecv.at[x, p], device(q, z, y, c)).start()
    for n, p in enumerate(far):
        onward(p)
        if n < NEAR:
            row = w_ref.at[:, near[n], c]
            remote(row, row, ysend, yrecv.at[near[n]], sib).wait_recv()
            share(near[n])
    half = w_ref.at[:, pl.ds(0, 4)]
    remote(half, half, csend, crecv, sib).wait()
    sent = w_ref.at[0, pl.ds(0, 7 - NEAR), 0]
    remote(sent, sent, ysend, yrecv.at[0], sib).wait_send()
    sent = w_ref.at[:, pl.ds(0, NEAR), 0]
    remote(sent, sent, nsend, yrecv.at[0], sib).wait_send()
    sent = w_ref.at[pl.ds(0, 3), pl.ds(0, 7 - NEAR), 0]
    remote(sent, sent, xsend, yrecv.at[0], sib).wait_send()


def main_kernel(
    w_ref, hid_hbm, gm_hbm, nb_ref, irms_ref, cos_ref, sin_ref, mask_ref,
    mixed_ref, gh_ref, gout_ref,
    hid_ref, gm_ref, pin, pout, cin, cout, xin, xout, xrin, xrout, yout, yrout, ybuf, yrbuf, msg, rbuf,
    cs, cr, xs, xr, ys, yr, fs, fr, ls, relay,
):
    x, z, y, c = coords()
    me = 2 * y + c
    sib = device(x, z, y, 1 - c)
    xpeers = [lax.rem(x + k, NX) for k in range(1, NX)]
    ypeers = [lax.rem(y + k, NY) for k in range(1, NY)]
    group, quad = lax.div(y, 4), lax.rem(y, 4)
    sy, sc = 4 * group + lax.div(lax.rem(z, 8), 2), lax.div(z, 8)
    diagonal = jnp.logical_and(sy == y, sc == c)
    barrier = pltpu.get_barrier_semaphore()
    signal(barrier, sib)
    for p in xpeers:
        signal(barrier, device(p, z, y, c))
    for p in ypeers:
        signal(barrier, device(x, z, p, c))
    for k in (1, 2, 3, 4, 12, 13, 14, 15):
        signal(barrier, device(x, lax.rem(z + k, NZ), y, c))
    gm_load = pltpu.make_async_copy(gm_hbm, gm_ref, ls.at[0])
    gm_load.start()
    hid_load = pltpu.make_async_copy(hid_hbm, hid_ref, ls.at[1])
    hid_load.start()

    lo = lanes((TOK, 128)) < 64
    cos, sin = cos_ref[...], sin_ref[...]
    grad_scale = 131072 ** (-0.5)
    zero = jnp.zeros((TOK, 128), F32)

    nb = nb_ref[...]
    proj = [jnp.dot(nb, w_ref[t], preferred_element_type=F32) for t in range(2)]
    proj.append(jnp.dot(nb, w_ref[2, :, :128], preferred_element_type=F32))
    q = []
    for t in range(4):
        v = proj[t // 2][:, 128 * (t % 2) : 128 * (t % 2) + 128]
        q.append(v * cos + swap_halves(v) * sin)
    k_hi = jnp.where(lo, zero, q[3])
    k_lo = pltpu.roll(k_hi, 64, 1)
    q[3] = jnp.where(lo, q[3], zero)
    qb = [v.astype(BF16) for v in q]
    kk = jnp.concatenate([k_lo.astype(BF16), k_hi.astype(BF16)], axis=0)
    v_lo = jnp.where(lo, proj[2], zero)
    v_hi = pltpu.roll(v_lo, 64, 1)
    vv = jnp.concatenate([v_lo.astype(BF16), v_hi.astype(BF16)], axis=0)
    allowed = mask_ref[...] > 0.5
    probs, pb = [], []
    for t in range(4):
        s2 = lax.dot_general(qb[t], kk if t < 3 else kk[:128], NT, preferred_element_type=F32)
        for h in range(2 if t < 3 else 1):
            s = jnp.where(allowed, s2[:, 128 * h : 128 * h + 128] * 0.125, -1e30)
            e = jnp.exp(s - jnp.max(s, axis=1, keepdims=True))
            p = e * (1.0 / jnp.sum(e, axis=1, keepdims=True))
            probs.append(p)
            pb.append(p.astype(BF16))
    att = [jnp.dot(pb[0], vv[128:], preferred_element_type=F32).astype(BF16)]
    for t in range(1, 4):
        pair = jnp.concatenate([pb[2 * t - 1], pb[2 * t]], axis=1)
        att.append(jnp.dot(pair, vv, preferred_element_type=F32).astype(BF16))
    a = jnp.concatenate(att, axis=1)
    gm_load.wait()
    gm = gm_ref[...]
    src, dst = lanes((512, 512), 0), lanes((512, 512))
    block = 7 * (2 * ((dst >> 5) & 3) + ((dst >> 2) & 1)) + 3 * ((dst >> 7) & 1) + (dst & 3)
    want = 64 + 112 * ((dst >> 3) & 3) + 56 * (dst >> 8) + block
    order = jnp.where(src == want, 1.0, 0.0).astype(BF16)
    ordered = jnp.dot(a, order, preferred_element_type=F32).astype(BF16)
    part = lax.dot_general(ordered, gm, TN, preferred_element_type=F32)
    for h in range(2):
        for p in range(NY):
            r = 256 * h + 32 * p
            pout[h, p] = (part[r : r + 32] * grad_scale).astype(BF16)
    pl.semaphore_wait(barrier, 19)
    copies = []
    for k in range(NY):
        p = lax.rem(y + 1 + k, NY)
        cp = remote(pout.at[1 - c, p], cout.at[p], cs.at[k], cr.at[p], sib)
        cp.start()
        copies.append(cp)

    ga = [jnp.dot(gm, w_ref[t], preferred_element_type=F32) for t in (2, 3)]
    g = [ga[t // 2][:, 128 * (t % 2) : 128 * (t % 2) + 128] for t in range(4)]
    g[0] = jnp.where(lo, zero, g[0])
    gb = [v.astype(BF16) for v in g]
    gs = [None] * 7
    for t in range(4):
        g2 = lax.dot_general(gb[t], vv if t > 0 else vv[128:], NT, preferred_element_type=F32)
        prod = gb[t].astype(F32) * att[t].astype(F32)
        for h in range(2 if t > 0 else 1):
            head = 2 * t - 1 + h if t > 0 else 0
            if t == 0:
                delta = jnp.sum(prod, axis=1, keepdims=True)
            else:
                delta = jnp.sum(jnp.where(lo, prod, zero) if h == 0 else jnp.where(lo, zero, prod), axis=1, keepdims=True)
            gp = g2[:, 128 * h : 128 * h + 128]
            gs[head] = (probs[head] * (gp - delta) * 0.125).astype(BF16)
    zb = jnp.zeros((TOK, 128), BF16)
    q_rows = [jnp.where(lo, q[h // 2], zero).astype(BF16) if h % 2 == 0 else jnp.where(lo, zero, q[h // 2]).astype(BF16) for h in range(7)]
    g_rows = [gb[0]] + [
        (jnp.where(lo, g[(h + 1) // 2], zero) if h % 2 == 1 else jnp.where(lo, zero, g[h // 2])).astype(BF16) for h in range(1, 7)
    ]
    gk = lax.dot_general(jnp.concatenate(gs, axis=0), jnp.concatenate(q_rows, axis=0), TN, preferred_element_type=F32)
    gk = gk + pltpu.roll(gk, 64, 1)
    gv = lax.dot_general(jnp.concatenate(pb, axis=0), jnp.concatenate(g_rows, axis=0), TN, preferred_element_type=F32)
    gv = gv + pltpu.roll(gv, 64, 1)
    tiles = []
    for t in range(4):
        if t < 3:
            pair = jnp.concatenate([gs[2 * t], gs[2 * t + 1]], axis=1)
            v = jnp.dot(pair, kk, preferred_element_type=F32)
        else:
            v = jnp.dot(gs[6], kk[:128], preferred_element_type=F32)
            v = jnp.where(lo, v, gk)
        tiles.append((v * cos - swap_halves(v) * sin).astype(BF16))
    tiles.append(jnp.where(lo, gv, zero).astype(BF16))
    gpa = jnp.concatenate(tiles, axis=1)
    part = lax.dot_general(nb, gpa, TN, preferred_element_type=F32)
    for h in range(2):
        for p in range(NX):
            r = 224 * p + 112 * h
            pin[h, p] = (part[r : r + 112] * grad_scale).astype(BF16)
    for k in range(NX):
        p = lax.rem(x + 1 + k, NX)
        cp = remote(pin.at[1 - c, p], cin.at[p], cs.at[8 + k], cr.at[8 + p], sib)
        cp.start()
        copies.append(cp)

    sum_out = sum_in = None
    for k in range(NY):
        p = lax.rem(y + 1 + k, NY)
        remote(pout.at[c, p], cout.at[p], cs.at[0], cr.at[p], sib).wait_recv()
        s = pout[c, p].astype(F32) + cout[p].astype(F32)
        if k < NY - 1:
            yout[k] = s.astype(BF16)
            cp = remote(yout.at[k], yrout.at[y], ys.at[8 + k], yr.at[8 + y], device(x, z, p, c))
            cp.start()
            copies.append(cp)
        else:
            sum_out = s
    for k in range(NX):
        p = lax.rem(x + 1 + k, NX)
        remote(pin.at[c, p], cin.at[p], cs.at[0], cr.at[8 + p], sib).wait_recv()
        s = pin[c, p].astype(F32) + cin[p].astype(F32)
        if k < NX - 1:
            xin[k] = s.astype(BF16)
            cp = remote(xin.at[k], xrin.at[x], xs.at[k], xr.at[x], device(p, z, y, c))
            cp.start()
            copies.append(cp)
        else:
            sum_in = s

    for k in range(2):
        up = device(x, lax.rem(z + 4 + 8 * k, NZ), y, c)
        pl.semaphore_signal(relay.at[k], inc=1, device_id=up, device_id_type=MESH)

    hid_load.wait()
    hid = hid_ref[...].astype(F32)
    out = sum(lax.dot_general(a[:, 256 * t : 256 * t + 256], w_ref[2 + t], NT, preferred_element_type=F32) for t in range(2))
    mixed_ref[...] = (hid + out).astype(BF16)
    gn = sum(lax.dot_general(gpa[:, 256 * t : 256 * t + 256], w_ref[t], NT, preferred_element_type=F32) for t in range(2))
    gn = gn + lax.dot_general(gpa[:, 512:], w_ref[2, :, :128], NT, preferred_element_type=F32)
    irms = irms_ref[:, :1]
    normed = hid * irms
    mean = jnp.mean(gn * normed, axis=1, keepdims=True)
    gh_ref[...] = ((gn - normed * mean) * irms + gm.astype(F32)).astype(BF16)

    row, col = lanes((128, 112), 0), lanes((128, 112))
    from_row = 14 * (2 * ((row >> 4) & 3) + ((row >> 3) & 1)) + 7 * (row >> 6) + (row & 7)
    e_in = jnp.where(((row & 7) < 7) & (col == from_row), 1.0, 0.0).astype(BF16)
    row, col = lanes((16, 16), 0), lanes((16, 16))
    turn = (row & 7) + group
    e_out = jnp.where(((row & 7) < 7) & (col == 4 * (row >> 3) + (turn >> 1) + 8 * (turn & 1)), 1.0, 0.0).astype(BF16)
    for p in xpeers:
        remote(xin.at[0], xrin.at[p], xs.at[0], xr.at[p], sib).wait_recv()
        sum_in = sum_in + xrin[p].astype(F32)
    y_in = jnp.dot(e_in, sum_in.astype(BF16), preferred_element_type=F32)
    for p in range(NY):
        ybuf[p] = y_in[16 * p : 16 * p + 16].astype(BF16)
    for k in range(2):
        pl.semaphore_wait(relay.at[k], 1)
    for k, p in enumerate(ypeers):
        cp = remote(ybuf.at[p], yrbuf.at[y], ys.at[k], yr.at[y], device(x, z, p, c))
        cp.start()
        copies.append(cp)

    for p in ypeers:
        remote(yout.at[0], yrout.at[p], ys.at[0], yr.at[8 + p], sib).wait_recv()
        sum_out = sum_out + yrout[p].astype(F32)
    for p in range(NX):
        xout[p] = sum_out[8 * p : 8 * p + 8]
    for k, p in enumerate(xpeers):
        cp = remote(xout.at[p], xrout.at[x], xs.at[4 + k], xr.at[4 + x], device(p, z, y, c))
        cp.start()
        copies.append(cp)
    sum_out = xout[x]
    for p in xpeers:
        remote(xout.at[0], xrout.at[p], xs.at[0], xr.at[4 + p], sib).wait_recv()
        sum_out = sum_out + xrout[p]
    left, right = sum_out[:, :512], pltpu.roll(sum_out[:, 384:], 448, 1)
    halves = jnp.concatenate([left, right], axis=0).astype(BF16)
    y_out = jnp.dot(e_out, halves, preferred_element_type=F32)
    before = pltpu.roll(y_out, 1, 0)
    lane, jrow = lanes((16, 512)), lanes((16, 512), 0) & 7
    flat_out = jnp.zeros((16, 512), F32)
    for k in range(8):
        old = lane < 56 * k + 120
        here, past = pltpu.roll(y_out, (120 + 56 * k) % 512, 1), pltpu.roll(before, (184 + 56 * k) % 512, 1)
        flat_out = jnp.where(jrow == k, jnp.where(old, past, here), flat_out)

    total = ybuf[y].astype(F32)
    for p in ypeers:
        remote(ybuf.at[0], yrbuf.at[p], ys.at[0], yr.at[p], sib).wait_recv()
        total = total + yrbuf[p].astype(F32)

    before = pltpu.roll(total, 1, 0)
    lane, jrow = lanes((16, 640)), lanes((16, 640), 0) & 7
    flat_in = jnp.zeros((16, 640), F32)
    for k in range(8):
        here, past = pltpu.roll(total, 72 * k, 1), pltpu.roll(before, 64 + 72 * k, 1)
        flat_in = jnp.where(jrow == k, jnp.where(lane < 72 * k, past, here), flat_in)
    seam = jnp.where(lanes((16, 128)) < 120, flat_in[:, 384:512], flat_out[:, :128])
    flat = jnp.concatenate([flat_in[:, :384], seam, flat_out[:, 128:], jnp.zeros((16, 128), F32)], axis=1)
    for t in range(8):
        msg[:, t, :] = flat[:, 128 * t : 128 * t + 128].astype(BF16)
    own = 8 * lax.rem(z, 2) + lax.rem(me, 8)

    def target(i):
        n = lax.rem(i, 8)
        return device(x, 8 * c + 2 * quad + lax.div(i, 8), 4 * group + lax.div(n, 2), lax.rem(n, 2))

    for k in range(1, 16):
        i = lax.rem(own + k, 16)
        cp = remote(msg.at[i], rbuf.at[z], fs.at[k], fr.at[z], target(i))
        cp.start()
        copies.append(cp)
    mine = remote(msg.at[own], rbuf.at[z], fs.at[0], fr.at[z], target(own))
    kept = pltpu.make_async_copy(msg.at[own], rbuf.at[z], ls.at[2])

    @pl.when(diagonal)
    def _():
        kept.start()
        kept.wait()

    @pl.when(jnp.logical_not(diagonal))
    def _():
        mine.start()
        mine.wait_send()
        remote(msg.at[0], rbuf.at[z], fs.at[0], fr.at[z], sib).wait_recv()

    for k in range(1, 16):
        s = lax.rem(z + k, 16)
        remote(msg.at[0], rbuf.at[s], fs.at[0], fr.at[s], sib).wait_recv()
    total = jnp.sum(rbuf[...].astype(F32), axis=0)
    for t in range(8):
        gout_ref[:, 128 * t : 128 * t + 128] = total[t : t + 1]
    for cp in copies:
        cp.wait_send()


def write_kernel(mixed_ref, gh_ref, grads_ref, mixed_out, gh_out, in_out, out_out, part_in, part_out, sem):
    pairs = ((mixed_ref, mixed_out), (gh_ref, gh_out), (part_in, in_out), (part_out, out_out))
    copies = [pltpu.make_async_copy(src, dst, sem.at[k]) for k, (src, dst) in enumerate(pairs)]
    for cp in copies[:2]:
        cp.start()
    flat = grads_ref[...]
    part_in[...] = flat[:, :504]
    part_out[...] = pltpu.roll(flat, 520, 1)[:, :392]
    for cp in copies[2:]:
        cp.start()
    for cp in copies:
        cp.wait()


def body(hidden_in, doc_ids, grad_mixed, in_codes, in_scales, out_codes, out_scales):
    vm = pl.BlockSpec(memory_space=VMEM)
    hbm = pl.BlockSpec(memory_space=pltpu.HBM)
    dma = pltpu.SemaphoreType.DMA
    sds = jax.ShapeDtypeStruct
    tokens = sds((TOK, D), BF16)
    square = sds((TOK, 128), F32)
    held = [pltpu.with_memory_space_constraint(v, pltpu.HBM) for v in (in_codes, out_codes.T, in_scales.T, out_scales, hidden_in, doc_ids)]
    grad_mixed = pltpu.with_memory_space_constraint(grad_mixed, pltpu.HBM)
    w, nb, irms, cos, sin, mask = pl.pallas_call(
        gather_kernel,
        out_shape=(sds((4, 8, 2, 56, 256), BF16), tokens, square, square, square, square),
        in_specs=[hbm] * 6,
        out_specs=(vm,) * 6,
        scratch_shapes=[
            VMEM((56, 576), BF16), VMEM((56, 448), BF16), VMEM((9, 28), F32), VMEM((7, 28), F32),
            VMEM((TOK, D), BF16), VMEM((1, 128), jnp.int32), VMEM((56, 128), F32),
            dma((6,)), dma, dma, dma((8,)), dma, dma((4, 8)), dma, dma,
        ],
        compiler_params=pltpu.CompilerParams(collective_id=0, has_side_effects=True, vmem_limit_bytes=16 << 20),
        name="gather",
    )(*held)
    mixed, grad_hidden, grads = pl.pallas_call(
        main_kernel,
        out_shape=(tokens, tokens, sds((1, 1024), F32)),
        in_specs=[vm, hbm, hbm] + [vm] * 5,
        out_specs=(vm, vm, vm),
        scratch_shapes=[
            VMEM((TOK, D), BF16), VMEM((TOK, D), BF16),
            VMEM((2, 4, 112, 640), BF16), VMEM((2, 8, 32, 896), BF16),
            VMEM((4, 112, 640), BF16), VMEM((8, 32, 896), BF16),
            VMEM((3, 112, 640), BF16), VMEM((4, 8, 896), F32),
            VMEM((4, 112, 640), BF16), VMEM((4, 8, 896), F32),
            VMEM((7, 32, 896), BF16), VMEM((8, 32, 896), BF16),
            VMEM((8, 16, 640), BF16), VMEM((8, 16, 640), BF16),
            VMEM((16, 8, 128), BF16), VMEM((16, 8, 128), BF16),
            dma((12,)), dma((12,)), dma((8,)), dma((8,)), dma((15,)), dma((16,)), dma((16,)), dma((16,)), dma((3,)), pltpu.SemaphoreType.REGULAR((2,)),
        ],
        compiler_params=pltpu.CompilerParams(collective_id=1, has_side_effects=True, vmem_limit_bytes=32 << 20),
        name="sublayer",
    )(w.reshape(4, D, 256), held[4], grad_mixed, nb, irms, cos, sin, mask)
    mixed, grad_hidden, grad_in, grad_out = pl.pallas_call(
        write_kernel,
        out_shape=(pltpu.HBM((TOK, D), BF16), pltpu.HBM((TOK, D), BF16), pltpu.HBM((1, 504), F32), pltpu.HBM((1, 392), F32)),
        in_specs=[vm] * 3,
        out_specs=(hbm,) * 4,
        scratch_shapes=[VMEM((1, 504), F32), VMEM((1, 392), F32), dma((4,))],
        name="write",
    )(*(pltpu.with_memory_space_constraint(v, VMEM) for v in (mixed, grad_hidden, grads)))
    return mixed, grad_hidden, grad_in.reshape(504), grad_out.reshape(392)


def solution(mesh):
    rows = P(("outer", "inner"), None)
    return jax.shard_map(
        body,
        mesh=mesh,
        in_specs=(rows, rows, rows, P("inner", None), P(), P(None, "inner"), P()),
        out_specs=(rows, rows, P(("outer", "inner")), P(("outer", "inner"))),
        check_vma=False,
    )
```

```python
import math

import jax
import jax.numpy as jnp
from jax import lax
from jax.experimental import pallas as pl
from jax.experimental.pallas import tpu as pltpu
from jax.sharding import PartitionSpec as P

MESH = pl.DeviceIdType.MESH
F32, BF16 = jnp.float32, jnp.bfloat16
D, HEADS, HS = 896, 7, 64
TOK = 128
NX, NZ, NY = 4, 16, 8
NEAR = 2
FAR_FIRST = (4, 3, 5, 2, 6, 1, 7)
ROPE_BASE = 1000000.0
EPS = 1e-06
VMEM = pltpu.VMEM
NT = (((1,), (1,)), ((), ()))
TN = (((0,), (0,)), ((), ()))


def coords():
    o = lax.axis_index("outer")
    i = lax.axis_index("inner")
    return lax.div(o, 16), lax.rem(o, 16), lax.div(i, 2), lax.rem(i, 2)


def device(x, z, y, c):
    return (x * 16 + z, y * 2 + c)


def signal(sem, dev):
    pl.semaphore_signal(sem, inc=1, device_id=dev, device_id_type=MESH)


def remote(src, dst, send, recv, dev):
    return pltpu.make_async_remote_copy(
        src_ref=src, dst_ref=dst, send_sem=send, recv_sem=recv, device_id=dev, device_id_type=MESH
    )


def lanes(shape, dim=1):
    return lax.broadcasted_iota(jnp.int32, shape, dim)


def swap_halves(v):
    low = (lanes(v.shape) & 63) < 32
    return jnp.where(low, pltpu.roll(v, 96, 1), pltpu.roll(v, 32, 1))


def allowed_pairs(doc_ref):
    row = jnp.broadcast_to(doc_ref[...].astype(F32), (TOK, TOK))
    return (row == row.T) & (lanes((TOK, TOK)) <= lanes((TOK, TOK), 0))


def gather_kernel(
    inc_ref, outc_ref, ins_ref, outs_ref, hid_ref, doc_ref,
    w_ref, nb_ref, nbt_ref, irms_ref, cos_ref, sin_ref, mask_ref,
    ic, oc, ins, outs, hid, doc, pad, lsem, ysend, nsend, yrecv, xsend, xrecv, csend, crecv,
):
    x, z, y, c = coords()
    me = 2 * y + c
    sib = device(x, z, y, 1 - c)
    xpeers = [lax.rem(x + k, NX) for k in (1, 3, 2)]
    ypeers = [lax.rem(y + k, NY) for k in (1, 7, 2, 6, 3, 5, 4)]
    near, far = ypeers[:NEAR], ypeers[NEAR:]
    barrier = pltpu.get_barrier_semaphore()
    for p in ypeers:
        signal(barrier, device(x, z, p, c))
    for p in xpeers:
        signal(barrier, device(p, z, y, c))
    signal(barrier, sib)
    pairs = ((inc_ref, ic), (outc_ref, oc), (ins_ref, ins), (outs_ref, outs), (doc_ref, doc), (hid_ref, hid))
    loads = [pltpu.make_async_copy(src, dst, lsem.at[k]) for k, (src, dst) in enumerate(pairs)]
    for cp in loads:
        cp.start()
    pad[...] = jnp.zeros((56, 128), F32)
    for cp in loads[:4]:
        cp.wait()

    shift = jnp.where(lanes((448, 512)) == lanes((448, 512), 0) + 64, 1.0, 0.0).astype(BF16)
    turned = jnp.dot(oc[...], shift, preferred_element_type=F32)
    block = (lanes((56, 28), 0) + 56 * me) >> 5
    pick = jnp.where(block == lanes((56, 28)), 1.0, 0.0)
    s_in = lax.dot_general(pick, ins[...], NT, precision=lax.Precision.HIGHEST, preferred_element_type=F32)
    s_out = lax.dot_general(pick, outs[...], NT, precision=lax.Precision.HIGHEST, preferred_element_type=F32)
    columns = [s_in[:, k : k + 1] for k in range(9)] + [s_out[:, k : k + 1] for k in range(7)]
    low = lanes((56, 128)) < 64
    pad[:, :64] = ic[:, 512:].astype(F32)
    for t in range(8):
        if t < 4:
            code = ic[:, 128 * t : 128 * t + 128].astype(F32)
        else:
            code = turned[:, 128 * t - 512 : 128 * t - 384]
            if t == 4:
                code = code + pad[...]
        scale = jnp.where(low, columns[2 * t], columns[2 * t + 1])
        w_ref[t // 2, y, c, :, 128 * (t % 2) : 128 * (t % 2) + 128] = (code * scale).astype(BF16)

    pl.semaphore_wait(barrier, 11)
    mine = w_ref.at[x, y, c]
    whole = w_ref.at[:, y, c]
    for p in far:
        remote(mine, mine, ysend, yrecv.at[y], device(x, z, p, c)).start()
    for p in near:
        remote(whole, whole, nsend, yrecv.at[y], device(x, z, p, c)).start()
    remote(whole, whole, csend, crecv, sib).start()

    loads[4].wait()
    loads[5].wait()
    rows = hid[...].astype(F32)
    irms = lax.rsqrt(jnp.mean(rows * rows, axis=1, keepdims=True) + EPS)
    normed = rows * irms
    nb_ref[...] = normed.astype(BF16)
    nbt_ref[...] = normed.T.astype(BF16)
    irms_ref[...] = jnp.broadcast_to(irms, (TOK, 128))
    mask = jnp.where(allowed_pairs(doc), 1.0, 0.0)
    mask_ref[...] = mask
    pos = jnp.sum(mask, axis=1, keepdims=True) - 1.0
    lane = lanes((TOK, 128))
    freq = jnp.exp((lane & 31).astype(F32) * (-2.0 * math.log(ROPE_BASE) / HS))
    angle = pos * freq
    cos_ref[...] = jnp.cos(angle)
    sine = jnp.sin(angle)
    sin_ref[...] = jnp.where((lane & 63) < 32, -sine, sine)

    def share(p):
        row = w_ref.at[:, p, c]
        remote(row, row, csend, crecv, sib).start()

    def onward(p):
        for q in xpeers:
            piece = w_ref.at[q, p, c]
            remote(piece, piece, xsend, xrecv.at[q, p], sib).wait_recv()
        share(p)

    for p in far:
        piece = w_ref.at[x, p, c]
        remote(piece, piece, ysend, yrecv.at[p], sib).wait_recv()
        for q in xpeers:
            remote(piece, piece, xsend, xrecv.at[x, p], device(q, z, y, c)).start()
    for n, p in enumerate(far):
        onward(p)
        if n < NEAR:
            row = w_ref.at[:, near[n], c]
            remote(row, row, ysend, yrecv.at[near[n]], sib).wait_recv()
            share(near[n])
    half = w_ref.at[:, pl.ds(0, 4)]
    remote(half, half, csend, crecv, sib).wait()
    sent = w_ref.at[0, pl.ds(0, 7 - NEAR), 0]
    remote(sent, sent, ysend, yrecv.at[0], sib).wait_send()
    sent = w_ref.at[:, pl.ds(0, NEAR), 0]
    remote(sent, sent, nsend, yrecv.at[0], sib).wait_send()
    sent = w_ref.at[pl.ds(0, 3), pl.ds(0, 7 - NEAR), 0]
    remote(sent, sent, xsend, yrecv.at[0], sib).wait_send()


def main_kernel(
    w_ref, hid_hbm, gm_hbm, nb_ref, nbt_ref, irms_ref, cos_ref, sin_ref, mask_ref,
    mixed_ref, gh_ref, gout_ref,
    hid_ref, gm_ref, pin, pout, cin, cout, xin, xout, xrin, xrout, yout, yrout, ybuf, yrbuf, msg, rbuf,
    cs, cr, xs, xr, ys, yr, fs, fr, ls, relay,
):
    x, z, y, c = coords()
    me = 2 * y + c
    sib = device(x, z, y, 1 - c)
    xpeers = [lax.rem(x + k, NX) for k in (2, 1, 3)]
    ypeers = [lax.rem(y + k, NY) for k in FAR_FIRST]
    group, quad = lax.div(y, 4), lax.rem(y, 4)
    sy, sc = 4 * group + lax.div(lax.rem(z, 8), 2), lax.div(z, 8)
    diagonal = jnp.logical_and(sy == y, sc == c)
    barrier = pltpu.get_barrier_semaphore()
    signal(barrier, sib)
    for p in xpeers:
        signal(barrier, device(p, z, y, c))
    for p in ypeers:
        signal(barrier, device(x, z, p, c))
    for k in (1, 2, 3, 4, 12, 13, 14, 15):
        signal(barrier, device(x, lax.rem(z + k, NZ), y, c))
    gm_load = pltpu.make_async_copy(gm_hbm, gm_ref, ls.at[0])
    gm_load.start()
    hid_load = pltpu.make_async_copy(hid_hbm, hid_ref, ls.at[1])
    hid_load.start()

    lo = lanes((TOK, 128)) < 64
    cos, sin = cos_ref[...], sin_ref[...]
    grad_scale = 131072 ** (-0.5)
    zero = jnp.zeros((TOK, 128), F32)

    nb = nb_ref[...]
    proj = [jnp.dot(nb, w_ref[t], preferred_element_type=F32) for t in range(2)]
    proj.append(jnp.dot(nb, w_ref[2, :, :128], preferred_element_type=F32))
    q = []
    for t in range(4):
        v = proj[t // 2][:, 128 * (t % 2) : 128 * (t % 2) + 128]
        q.append(v * cos + swap_halves(v) * sin)
    k_hi = jnp.where(lo, zero, q[3])
    k_lo = pltpu.roll(k_hi, 64, 1)
    q[3] = jnp.where(lo, q[3], zero)
    qb = [v.astype(BF16) for v in q]
    kk = jnp.concatenate([k_lo.astype(BF16), k_hi.astype(BF16)], axis=0)
    v_lo = jnp.where(lo, proj[2], zero)
    v_hi = pltpu.roll(v_lo, 64, 1)
    vv = jnp.concatenate([v_lo.astype(BF16), v_hi.astype(BF16)], axis=0)
    allowed = mask_ref[...] > 0.5
    probs, pb = [], []
    for t in range(4):
        s2 = lax.dot_general(qb[t], kk if t < 3 else kk[:128], NT, preferred_element_type=F32)
        for h in range(2 if t < 3 else 1):
            s = jnp.where(allowed, s2[:, 128 * h : 128 * h + 128] * 0.125, -1e30)
            e = jnp.exp(s - jnp.max(s, axis=1, keepdims=True))
            p = e * (1.0 / jnp.sum(e, axis=1, keepdims=True))
            probs.append(p)
            pb.append(p.astype(BF16))
    att = [jnp.dot(pb[0], vv[128:], preferred_element_type=F32).astype(BF16)]
    for t in range(1, 4):
        pair = jnp.concatenate([pb[2 * t - 1], pb[2 * t]], axis=1)
        att.append(jnp.dot(pair, vv, preferred_element_type=F32).astype(BF16))
    a = jnp.concatenate(att, axis=1)
    gm_load.wait()
    gm = gm_ref[...]
    src, dst = lanes((512, 512), 0), lanes((512, 512))
    block = 7 * (2 * ((dst >> 5) & 3) + ((dst >> 2) & 1)) + 3 * ((dst >> 7) & 1) + (dst & 3)
    want = 64 + 112 * ((dst >> 3) & 3) + 56 * (dst >> 8) + block
    order = jnp.where(src == want, 1.0, 0.0).astype(BF16)
    ordered = jnp.dot(a, order, preferred_element_type=F32).astype(BF16)
    part = lax.dot_general(ordered, gm, TN, preferred_element_type=F32)
    for h in range(2):
        for p in range(NY):
            r = 256 * h + 32 * p
            pout[h, p] = (part[r : r + 32] * grad_scale).astype(BF16)
    pl.semaphore_wait(barrier, 19)
    copies = []
    for k, step in enumerate(FAR_FIRST + (0,)):
        p = lax.rem(y + step, NY)
        cp = remote(pout.at[1 - c, p], cout.at[p], cs.at[k], cr.at[p], sib)
        cp.start()
        copies.append(cp)

    ga = [jnp.dot(gm, w_ref[t], preferred_element_type=F32) for t in (2, 3)]
    g = [ga[t // 2][:, 128 * (t % 2) : 128 * (t % 2) + 128] for t in range(4)]
    g[0] = jnp.where(lo, zero, g[0])
    gb = [v.astype(BF16) for v in g]
    gs = [None] * 7
    for t in range(4):
        g2 = lax.dot_general(gb[t], vv if t > 0 else vv[128:], NT, preferred_element_type=F32)
        prod = gb[t].astype(F32) * att[t].astype(F32)
        for h in range(2 if t > 0 else 1):
            head = 2 * t - 1 + h if t > 0 else 0
            if t == 0:
                delta = jnp.sum(prod, axis=1, keepdims=True)
            else:
                delta = jnp.sum(jnp.where(lo, prod, zero) if h == 0 else jnp.where(lo, zero, prod), axis=1, keepdims=True)
            gp = g2[:, 128 * h : 128 * h + 128]
            gs[head] = (probs[head] * (gp - delta) * 0.125).astype(BF16)
    zb = jnp.zeros((TOK, 128), BF16)
    q_rows = [jnp.where(lo, q[h // 2], zero).astype(BF16) if h % 2 == 0 else jnp.where(lo, zero, q[h // 2]).astype(BF16) for h in range(7)]
    g_rows = [gb[0]] + [
        (jnp.where(lo, g[(h + 1) // 2], zero) if h % 2 == 1 else jnp.where(lo, zero, g[h // 2])).astype(BF16) for h in range(1, 7)
    ]
    gk = lax.dot_general(jnp.concatenate(gs, axis=0), jnp.concatenate(q_rows, axis=0), TN, preferred_element_type=F32)
    gk = gk + pltpu.roll(gk, 64, 1)
    gv = lax.dot_general(jnp.concatenate(pb, axis=0), jnp.concatenate(g_rows, axis=0), TN, preferred_element_type=F32)
    gv = gv + pltpu.roll(gv, 64, 1)
    tiles = []
    for t in range(4):
        if t < 3:
            pair = jnp.concatenate([gs[2 * t], gs[2 * t + 1]], axis=1)
            v = jnp.dot(pair, kk, preferred_element_type=F32)
        else:
            v = jnp.dot(gs[6], kk[:128], preferred_element_type=F32)
            v = jnp.where(lo, v, gk)
        tiles.append((v * cos - swap_halves(v) * sin).astype(BF16))
    tiles.append(jnp.where(lo, gv, zero).astype(BF16))
    gpa = jnp.concatenate(tiles, axis=1)
    for p in range(NX):
        part = jnp.dot(nbt_ref[224 * p : 224 * p + 224], gpa, preferred_element_type=F32)
        for h in range(2):
            pin[h, p] = (part[112 * h : 112 * h + 112] * grad_scale).astype(BF16)
        cp = remote(pin.at[1 - c, p], cin.at[p], cs.at[8 + p], cr.at[8 + p], sib)
        cp.start()
        copies.append(cp)

    sum_out = sum_in = None
    for k, step in enumerate(FAR_FIRST + (0,)):
        p = lax.rem(y + step, NY)
        remote(pout.at[c, p], cout.at[p], cs.at[0], cr.at[p], sib).wait_recv()
        s = pout[c, p].astype(F32) + cout[p].astype(F32)
        if k < NY - 1:
            yout[k] = s.astype(BF16)
            cp = remote(yout.at[k], yrout.at[y], ys.at[8 + k], yr.at[8 + y], device(x, z, p, c))
            cp.start()
            copies.append(cp)
        else:
            sum_out = s
    for k in range(NX):
        p = lax.rem(x + 1 + k, NX)
        remote(pin.at[c, p], cin.at[p], cs.at[0], cr.at[8 + p], sib).wait_recv()
        s = pin[c, p].astype(F32) + cin[p].astype(F32)
        if k < NX - 1:
            xin[k] = s.astype(BF16)
            cp = remote(xin.at[k], xrin.at[x], xs.at[k], xr.at[x], device(p, z, y, c))
            cp.start()
            copies.append(cp)
        else:
            sum_in = s

    for k in range(2):
        up = device(x, lax.rem(z + 4 + 8 * k, NZ), y, c)
        pl.semaphore_signal(relay.at[k], inc=1, device_id=up, device_id_type=MESH)

    hid_load.wait()
    hid = hid_ref[...].astype(F32)
    out = sum(lax.dot_general(a[:, 256 * t : 256 * t + 256], w_ref[2 + t], NT, preferred_element_type=F32) for t in range(2))
    mixed_ref[...] = (hid + out).astype(BF16)
    gn = sum(lax.dot_general(gpa[:, 256 * t : 256 * t + 256], w_ref[t], NT, preferred_element_type=F32) for t in range(2))
    gn = gn + lax.dot_general(gpa[:, 512:], w_ref[2, :, :128], NT, preferred_element_type=F32)
    irms = irms_ref[:, :1]
    normed = hid * irms
    mean = jnp.mean(gn * normed, axis=1, keepdims=True)
    gh_ref[...] = ((gn - normed * mean) * irms + gm.astype(F32)).astype(BF16)

    row, col = lanes((128, 112), 0), lanes((128, 112))
    from_row = 14 * (2 * ((row >> 4) & 3) + ((row >> 3) & 1)) + 7 * (row >> 6) + (row & 7)
    e_in = jnp.where(((row & 7) < 7) & (col == from_row), 1.0, 0.0).astype(BF16)
    row, col = lanes((16, 16), 0), lanes((16, 16))
    turn = (row & 7) + group
    e_out = jnp.where(((row & 7) < 7) & (col == 4 * (row >> 3) + (turn >> 1) + 8 * (turn & 1)), 1.0, 0.0).astype(BF16)
    for p in xpeers:
        remote(xin.at[0], xrin.at[p], xs.at[0], xr.at[p], sib).wait_recv()
        sum_in = sum_in + xrin[p].astype(F32)
    y_in = jnp.dot(e_in, sum_in.astype(BF16), preferred_element_type=F32)
    for p in range(NY):
        ybuf[p] = y_in[16 * p : 16 * p + 16].astype(BF16)
    for k in range(2):
        pl.semaphore_wait(relay.at[k], 1)
    for k, p in enumerate(ypeers):
        cp = remote(ybuf.at[p], yrbuf.at[y], ys.at[k], yr.at[y], device(x, z, p, c))
        cp.start()
        copies.append(cp)

    for p in ypeers:
        remote(yout.at[0], yrout.at[p], ys.at[0], yr.at[8 + p], sib).wait_recv()
        sum_out = sum_out + yrout[p].astype(F32)
    for p in range(NX):
        xout[p] = sum_out[8 * p : 8 * p + 8]
    for k, p in enumerate(xpeers):
        cp = remote(xout.at[p], xrout.at[x], xs.at[4 + k], xr.at[4 + x], device(p, z, y, c))
        cp.start()
        copies.append(cp)
    sum_out = xout[x]
    for p in xpeers:
        remote(xout.at[0], xrout.at[p], xs.at[0], xr.at[4 + p], sib).wait_recv()
        sum_out = sum_out + xrout[p]
    left, right = sum_out[:, :512], pltpu.roll(sum_out[:, 384:], 448, 1)
    halves = jnp.concatenate([left, right], axis=0).astype(BF16)
    y_out = jnp.dot(e_out, halves, preferred_element_type=F32)
    before = pltpu.roll(y_out, 1, 0)
    lane, jrow = lanes((16, 512)), lanes((16, 512), 0) & 7
    flat_out = jnp.zeros((16, 512), F32)
    for k in range(8):
        old = lane < 56 * k + 120
        here, past = pltpu.roll(y_out, (120 + 56 * k) % 512, 1), pltpu.roll(before, (184 + 56 * k) % 512, 1)
        flat_out = jnp.where(jrow == k, jnp.where(old, past, here), flat_out)

    total = ybuf[y].astype(F32)
    for p in ypeers:
        remote(ybuf.at[0], yrbuf.at[p], ys.at[0], yr.at[p], sib).wait_recv()
        total = total + yrbuf[p].astype(F32)

    before = pltpu.roll(total, 1, 0)
    lane, jrow = lanes((16, 640)), lanes((16, 640), 0) & 7
    flat_in = jnp.zeros((16, 640), F32)
    for k in range(8):
        here, past = pltpu.roll(total, 72 * k, 1), pltpu.roll(before, 64 + 72 * k, 1)
        flat_in = jnp.where(jrow == k, jnp.where(lane < 72 * k, past, here), flat_in)
    seam = jnp.where(lanes((16, 128)) < 120, flat_in[:, 384:512], flat_out[:, :128])
    flat = jnp.concatenate([flat_in[:, :384], seam, flat_out[:, 128:], jnp.zeros((16, 128), F32)], axis=1)
    for t in range(8):
        msg[:, t, :] = flat[:, 128 * t : 128 * t + 128].astype(BF16)
    own = 8 * lax.rem(z, 2) + lax.rem(me, 8)

    def target(i):
        n = lax.rem(i, 8)
        return device(x, 8 * c + 2 * quad + lax.div(i, 8), 4 * group + lax.div(n, 2), lax.rem(n, 2))

    for k in range(1, 16):
        i = lax.rem(own + k, 16)
        cp = remote(msg.at[i], rbuf.at[z], fs.at[k], fr.at[z], target(i))
        cp.start()
        copies.append(cp)
    mine = remote(msg.at[own], rbuf.at[z], fs.at[0], fr.at[z], target(own))
    kept = pltpu.make_async_copy(msg.at[own], rbuf.at[z], ls.at[2])

    @pl.when(diagonal)
    def _():
        kept.start()
        kept.wait()

    @pl.when(jnp.logical_not(diagonal))
    def _():
        mine.start()
        mine.wait_send()
        remote(msg.at[0], rbuf.at[z], fs.at[0], fr.at[z], sib).wait_recv()

    for k in range(1, 16):
        s = lax.rem(z + k, 16)
        remote(msg.at[0], rbuf.at[s], fs.at[0], fr.at[s], sib).wait_recv()
    total = jnp.sum(rbuf[...].astype(F32), axis=0)
    for t in range(8):
        gout_ref[:, 128 * t : 128 * t + 128] = total[t : t + 1]
    for cp in copies:
        cp.wait_send()


def write_kernel(mixed_ref, gh_ref, grads_ref, mixed_out, gh_out, in_out, out_out, part_in, part_out, sem):
    pairs = ((mixed_ref, mixed_out), (gh_ref, gh_out), (part_in, in_out), (part_out, out_out))
    copies = [pltpu.make_async_copy(src, dst, sem.at[k]) for k, (src, dst) in enumerate(pairs)]
    for cp in copies[:2]:
        cp.start()
    flat = grads_ref[...]
    part_in[...] = flat[:, :504]
    part_out[...] = pltpu.roll(flat, 520, 1)[:, :392]
    for cp in copies[2:]:
        cp.start()
    for cp in copies:
        cp.wait()


def body(hidden_in, doc_ids, grad_mixed, in_codes, in_scales, out_codes, out_scales):
    vm = pl.BlockSpec(memory_space=VMEM)
    hbm = pl.BlockSpec(memory_space=pltpu.HBM)
    dma = pltpu.SemaphoreType.DMA
    sds = jax.ShapeDtypeStruct
    tokens = sds((TOK, D), BF16)
    square = sds((TOK, 128), F32)
    held = [pltpu.with_memory_space_constraint(v, pltpu.HBM) for v in (in_codes, out_codes.T, in_scales.T, out_scales, hidden_in, doc_ids)]
    grad_mixed = pltpu.with_memory_space_constraint(grad_mixed, pltpu.HBM)
    w, *rest = pl.pallas_call(
        gather_kernel,
        out_shape=(sds((4, 8, 2, 56, 256), BF16), tokens, sds((D, TOK), BF16), square, square, square, square),
        in_specs=[hbm] * 6,
        out_specs=(vm,) * 7,
        scratch_shapes=[
            VMEM((56, 576), BF16), VMEM((56, 448), BF16), VMEM((9, 28), F32), VMEM((7, 28), F32),
            VMEM((TOK, D), BF16), VMEM((1, 128), jnp.int32), VMEM((56, 128), F32),
            dma((6,)), dma, dma, dma((8,)), dma, dma((4, 8)), dma, dma,
        ],
        compiler_params=pltpu.CompilerParams(collective_id=0, has_side_effects=True, vmem_limit_bytes=16 << 20),
        name="gather",
    )(*held)
    mixed, grad_hidden, grads = pl.pallas_call(
        main_kernel,
        out_shape=(tokens, tokens, sds((1, 1024), F32)),
        in_specs=[vm, hbm, hbm] + [vm] * 6,
        out_specs=(vm, vm, vm),
        scratch_shapes=[
            VMEM((TOK, D), BF16), VMEM((TOK, D), BF16),
            VMEM((2, 4, 112, 640), BF16), VMEM((2, 8, 32, 896), BF16),
            VMEM((4, 112, 640), BF16), VMEM((8, 32, 896), BF16),
            VMEM((3, 112, 640), BF16), VMEM((4, 8, 896), F32),
            VMEM((4, 112, 640), BF16), VMEM((4, 8, 896), F32),
            VMEM((7, 32, 896), BF16), VMEM((8, 32, 896), BF16),
            VMEM((8, 16, 640), BF16), VMEM((8, 16, 640), BF16),
            VMEM((16, 8, 128), BF16), VMEM((16, 8, 128), BF16),
            dma((12,)), dma((12,)), dma((8,)), dma((8,)), dma((15,)), dma((16,)), dma((16,)), dma((16,)), dma((3,)), pltpu.SemaphoreType.REGULAR((2,)),
        ],
        compiler_params=pltpu.CompilerParams(collective_id=1, has_side_effects=True, vmem_limit_bytes=32 << 20),
        name="sublayer",
    )(w.reshape(4, D, 256), held[4], grad_mixed, *rest)
    mixed, grad_hidden, grad_in, grad_out = pl.pallas_call(
        write_kernel,
        out_shape=(pltpu.HBM((TOK, D), BF16), pltpu.HBM((TOK, D), BF16), pltpu.HBM((1, 504), F32), pltpu.HBM((1, 392), F32)),
        in_specs=[vm] * 3,
        out_specs=(hbm,) * 4,
        scratch_shapes=[VMEM((1, 504), F32), VMEM((1, 392), F32), dma((4,))],
        name="write",
    )(*(pltpu.with_memory_space_constraint(v, VMEM) for v in (mixed, grad_hidden, grads)))
    return mixed, grad_hidden, grad_in.reshape(504), grad_out.reshape(392)


def solution(mesh):
    rows = P(("outer", "inner"), None)
    return jax.shard_map(
        body,
        mesh=mesh,
        in_specs=(rows, rows, rows, P("inner", None), P(), P(None, "inner"), P()),
        out_specs=(rows, rows, P(("outer", "inner")), P(("outer", "inner"))),
        check_vma=False,
    )
```

```python
import math

import jax
import jax.numpy as jnp
from jax import lax
from jax.experimental import pallas as pl
from jax.experimental.pallas import tpu as pltpu
from jax.sharding import PartitionSpec as P

MESH = pl.DeviceIdType.MESH
F32, BF16 = jnp.float32, jnp.bfloat16
D, HEADS, HS = 896, 7, 64
TOK = 128
NX, NZ, NY = 4, 16, 8
NEAR = 2
FAR_FIRST = (4, 3, 5, 2, 6, 1, 7)
ROPE_BASE = 1000000.0
EPS = 1e-06
VMEM = pltpu.VMEM
NT = (((1,), (1,)), ((), ()))
TN = (((0,), (0,)), ((), ()))


def coords():
    o = lax.axis_index("outer")
    i = lax.axis_index("inner")
    return lax.div(o, 16), lax.rem(o, 16), lax.div(i, 2), lax.rem(i, 2)


def device(x, z, y, c):
    return (x * 16 + z, y * 2 + c)


def signal(sem, dev):
    pl.semaphore_signal(sem, inc=1, device_id=dev, device_id_type=MESH)


def remote(src, dst, send, recv, dev):
    return pltpu.make_async_remote_copy(
        src_ref=src, dst_ref=dst, send_sem=send, recv_sem=recv, device_id=dev, device_id_type=MESH
    )


def lanes(shape, dim=1):
    return lax.broadcasted_iota(jnp.int32, shape, dim)


def swap_halves(v):
    low = (lanes(v.shape) & 63) < 32
    return jnp.where(low, pltpu.roll(v, 96, 1), pltpu.roll(v, 32, 1))


def allowed_pairs(doc_ref):
    row = jnp.broadcast_to(doc_ref[...].astype(F32), (TOK, TOK))
    return (row == row.T) & (lanes((TOK, TOK)) <= lanes((TOK, TOK), 0))


def gather_kernel(
    inc_ref, outc_ref, ins_ref, outs_ref, hid_ref, doc_ref,
    w_ref, nb_ref, nbt_ref, irms_ref, cos_ref, sin_ref, mask_ref,
    ic, oc, ins, outs, hid, doc, pad, lsem, ysend, nsend, yrecv, xsend, xrecv, csend, crecv,
):
    x, z, y, c = coords()
    me = 2 * y + c
    sib = device(x, z, y, 1 - c)
    xpeers = [lax.rem(x + k, NX) for k in (1, 3, 2)]
    ypeers = [lax.rem(y + k, NY) for k in (1, 7, 2, 6, 3, 5, 4)]
    near, far = ypeers[:NEAR], ypeers[NEAR:]
    barrier = pltpu.get_barrier_semaphore()
    for p in ypeers:
        signal(barrier, device(x, z, p, c))
    for p in xpeers:
        signal(barrier, device(p, z, y, c))
    signal(barrier, sib)
    pairs = ((inc_ref, ic), (outc_ref, oc), (ins_ref, ins), (outs_ref, outs), (doc_ref, doc), (hid_ref, hid))
    loads = [pltpu.make_async_copy(src, dst, lsem.at[k]) for k, (src, dst) in enumerate(pairs)]
    for cp in loads:
        cp.start()
    pad[...] = jnp.zeros((56, 128), F32)
    for cp in loads[:4]:
        cp.wait()

    shift = jnp.where(lanes((448, 512)) == lanes((448, 512), 0) + 64, 1.0, 0.0).astype(BF16)
    turned = jnp.dot(oc[...], shift, preferred_element_type=F32)
    block = (lanes((56, 28), 0) + 56 * me) >> 5
    pick = jnp.where(block == lanes((56, 28)), 1.0, 0.0)
    s_in = lax.dot_general(pick, ins[...], NT, precision=lax.Precision.HIGHEST, preferred_element_type=F32)
    s_out = lax.dot_general(pick, outs[...], NT, precision=lax.Precision.HIGHEST, preferred_element_type=F32)
    columns = [s_in[:, k : k + 1] for k in range(9)] + [s_out[:, k : k + 1] for k in range(7)]
    low = lanes((56, 128)) < 64
    pad[:, :64] = ic[:, 512:].astype(F32)
    for t in range(8):
        if t < 4:
            code = ic[:, 128 * t : 128 * t + 128].astype(F32)
        else:
            code = turned[:, 128 * t - 512 : 128 * t - 384]
            if t == 4:
                code = code + pad[...]
        scale = jnp.where(low, columns[2 * t], columns[2 * t + 1])
        w_ref[t // 2, y, c, :, 128 * (t % 2) : 128 * (t % 2) + 128] = (code * scale).astype(BF16)

    pl.semaphore_wait(barrier, 11)
    mine = w_ref.at[x, y, c]
    whole = w_ref.at[:, y, c]
    for p in far:
        remote(mine, mine, ysend, yrecv.at[y], device(x, z, p, c)).start()
    for p in near:
        remote(whole, whole, nsend, yrecv.at[y], device(x, z, p, c)).start()
    remote(whole, whole, csend, crecv, sib).start()

    loads[4].wait()
    loads[5].wait()
    rows = hid[...].astype(F32)
    irms = lax.rsqrt(jnp.mean(rows * rows, axis=1, keepdims=True) + EPS)
    normed = rows * irms
    nb_ref[...] = normed.astype(BF16)
    nbt_ref[...] = normed.T.astype(BF16)
    irms_ref[...] = jnp.broadcast_to(irms, (TOK, 128))
    mask = jnp.where(allowed_pairs(doc), 1.0, 0.0)
    mask_ref[...] = mask
    pos = jnp.sum(mask, axis=1, keepdims=True) - 1.0
    lane = lanes((TOK, 128))
    freq = jnp.exp((lane & 31).astype(F32) * (-2.0 * math.log(ROPE_BASE) / HS))
    angle = pos * freq
    cos_ref[...] = jnp.cos(angle)
    sine = jnp.sin(angle)
    sin_ref[...] = jnp.where((lane & 63) < 32, -sine, sine)

    def share(p):
        row = w_ref.at[:, p, c]
        remote(row, row, csend, crecv, sib).start()

    def onward(p):
        for q in xpeers:
            piece = w_ref.at[q, p, c]
            remote(piece, piece, xsend, xrecv.at[q, p], sib).wait_recv()
        share(p)

    for p in far:
        piece = w_ref.at[x, p, c]
        remote(piece, piece, ysend, yrecv.at[p], sib).wait_recv()
        for q in xpeers:
            remote(piece, piece, xsend, xrecv.at[x, p], device(q, z, y, c)).start()
    for n, p in enumerate(far):
        onward(p)
        if n < NEAR:
            row = w_ref.at[:, near[n], c]
            remote(row, row, ysend, yrecv.at[near[n]], sib).wait_recv()
            share(near[n])
    half = w_ref.at[:, pl.ds(0, 4)]
    remote(half, half, csend, crecv, sib).wait()
    sent = w_ref.at[0, pl.ds(0, 7 - NEAR), 0]
    remote(sent, sent, ysend, yrecv.at[0], sib).wait_send()
    sent = w_ref.at[:, pl.ds(0, NEAR), 0]
    remote(sent, sent, nsend, yrecv.at[0], sib).wait_send()
    sent = w_ref.at[pl.ds(0, 3), pl.ds(0, 7 - NEAR), 0]
    remote(sent, sent, xsend, yrecv.at[0], sib).wait_send()


def main_kernel(
    w_ref, hid_hbm, gm_hbm, nb_ref, nbt_ref, irms_ref, cos_ref, sin_ref, mask_ref,
    mixed_ref, gh_ref, gout_ref,
    hid_ref, gm_ref, pin, pout, cin, cout, xin, xout, xrin, xrout, yout, yrout, ybuf, yrbuf, msg, rbuf,
    cs, cr, xs, xr, ys, yr, fs, fr, ls, relay,
):
    x, z, y, c = coords()
    me = 2 * y + c
    sib = device(x, z, y, 1 - c)
    xpeers = [lax.rem(x + k, NX) for k in (2, 1, 3)]
    ypeers = [lax.rem(y + k, NY) for k in FAR_FIRST]
    group, quad = lax.div(y, 4), lax.rem(y, 4)
    sy, sc = 4 * group + lax.div(lax.rem(z, 8), 2), lax.div(z, 8)
    diagonal = jnp.logical_and(sy == y, sc == c)
    barrier = pltpu.get_barrier_semaphore()
    signal(barrier, sib)
    for p in xpeers:
        signal(barrier, device(p, z, y, c))
    for p in ypeers:
        signal(barrier, device(x, z, p, c))
    for k in (1, 2, 3, 4, 12, 13, 14, 15):
        signal(barrier, device(x, lax.rem(z + k, NZ), y, c))
    gm_load = pltpu.make_async_copy(gm_hbm, gm_ref, ls.at[0])
    gm_load.start()
    hid_load = pltpu.make_async_copy(hid_hbm, hid_ref, ls.at[1])
    hid_load.start()

    lo = lanes((TOK, 128)) < 64
    cos, sin = cos_ref[...], sin_ref[...]
    grad_scale = 131072 ** (-0.5)
    zero = jnp.zeros((TOK, 128), F32)

    nb = nb_ref[...]
    proj = [jnp.dot(nb, w_ref[t], preferred_element_type=F32) for t in range(2)]
    proj.append(jnp.dot(nb, w_ref[2, :, :128], preferred_element_type=F32))
    q = []
    for t in range(4):
        v = proj[t // 2][:, 128 * (t % 2) : 128 * (t % 2) + 128]
        q.append(v * cos + swap_halves(v) * sin)
    k_hi = jnp.where(lo, zero, q[3])
    k_lo = pltpu.roll(k_hi, 64, 1)
    q[3] = jnp.where(lo, q[3], zero)
    qb = [v.astype(BF16) for v in q]
    kk = jnp.concatenate([k_lo.astype(BF16), k_hi.astype(BF16)], axis=0)
    v_lo = jnp.where(lo, proj[2], zero)
    v_hi = pltpu.roll(v_lo, 64, 1)
    vv = jnp.concatenate([v_lo.astype(BF16), v_hi.astype(BF16)], axis=0)
    allowed = mask_ref[...] > 0.5
    probs, pb = [], []
    for t in range(4):
        s2 = lax.dot_general(qb[t], kk if t < 3 else kk[:128], NT, preferred_element_type=F32)
        for h in range(2 if t < 3 else 1):
            s = jnp.where(allowed, s2[:, 128 * h : 128 * h + 128] * 0.125, -1e30)
            e = jnp.exp(s - jnp.max(s, axis=1, keepdims=True))
            p = e * (1.0 / jnp.sum(e, axis=1, keepdims=True))
            probs.append(p)
            pb.append(p.astype(BF16))
    att = [jnp.dot(pb[0], vv[128:], preferred_element_type=F32).astype(BF16)]
    for t in range(1, 4):
        pair = jnp.concatenate([pb[2 * t - 1], pb[2 * t]], axis=1)
        att.append(jnp.dot(pair, vv, preferred_element_type=F32).astype(BF16))
    a = jnp.concatenate(att, axis=1)
    gm_load.wait()
    gm = gm_ref[...]
    src, dst = lanes((512, 512), 0), lanes((512, 512))
    block = 7 * (2 * ((dst >> 5) & 3) + ((dst >> 2) & 1)) + 3 * ((dst >> 7) & 1) + (dst & 3)
    want = 64 + 112 * ((dst >> 3) & 3) + 56 * (dst >> 8) + block
    order = jnp.where(src == want, 1.0, 0.0).astype(BF16)
    ordered = jnp.dot(a, order, preferred_element_type=F32).astype(BF16)
    part = lax.dot_general(ordered, gm, TN, preferred_element_type=F32)
    for h in range(2):
        for p in range(NY):
            r = 256 * h + 32 * p
            pout[h, p] = (part[r : r + 32] * grad_scale).astype(BF16)
    pl.semaphore_wait(barrier, 19)
    copies = []
    for k, step in enumerate(FAR_FIRST + (0,)):
        p = lax.rem(y + step, NY)
        cp = remote(pout.at[1 - c, p], cout.at[p], cs.at[k], cr.at[p], sib)
        cp.start()
        copies.append(cp)

    ga = [jnp.dot(gm, w_ref[t], preferred_element_type=F32) for t in (2, 3)]
    g = [ga[t // 2][:, 128 * (t % 2) : 128 * (t % 2) + 128] for t in range(4)]
    g[0] = jnp.where(lo, zero, g[0])
    gb = [v.astype(BF16) for v in g]
    gs = [None] * 7
    for t in range(4):
        g2 = lax.dot_general(gb[t], vv if t > 0 else vv[128:], NT, preferred_element_type=F32)
        prod = gb[t].astype(F32) * att[t].astype(F32)
        for h in range(2 if t > 0 else 1):
            head = 2 * t - 1 + h if t > 0 else 0
            if t == 0:
                delta = jnp.sum(prod, axis=1, keepdims=True)
            else:
                delta = jnp.sum(jnp.where(lo, prod, zero) if h == 0 else jnp.where(lo, zero, prod), axis=1, keepdims=True)
            gp = g2[:, 128 * h : 128 * h + 128]
            gs[head] = (probs[head] * (gp - delta) * 0.125).astype(BF16)
    zb = jnp.zeros((TOK, 128), BF16)
    q_rows = [jnp.where(lo, q[h // 2], zero).astype(BF16) if h % 2 == 0 else jnp.where(lo, zero, q[h // 2]).astype(BF16) for h in range(7)]
    g_rows = [gb[0]] + [
        (jnp.where(lo, g[(h + 1) // 2], zero) if h % 2 == 1 else jnp.where(lo, zero, g[h // 2])).astype(BF16) for h in range(1, 7)
    ]
    gk = lax.dot_general(jnp.concatenate(gs, axis=0), jnp.concatenate(q_rows, axis=0), TN, preferred_element_type=F32)
    gk = gk + pltpu.roll(gk, 64, 1)
    gv = lax.dot_general(jnp.concatenate(pb, axis=0), jnp.concatenate(g_rows, axis=0), TN, preferred_element_type=F32)
    gv = gv + pltpu.roll(gv, 64, 1)
    tiles = []
    for t in range(4):
        if t < 3:
            pair = jnp.concatenate([gs[2 * t], gs[2 * t + 1]], axis=1)
            v = jnp.dot(pair, kk, preferred_element_type=F32)
        else:
            v = jnp.dot(gs[6], kk[:128], preferred_element_type=F32)
            v = jnp.where(lo, v, gk)
        tiles.append((v * cos - swap_halves(v) * sin).astype(BF16))
    tiles.append(jnp.where(lo, gv, zero).astype(BF16))
    gpa = jnp.concatenate(tiles, axis=1)
    for p in range(NX):
        part = jnp.dot(nbt_ref[224 * p : 224 * p + 224], gpa, preferred_element_type=F32)
        for h in range(2):
            pin[h, p] = (part[112 * h : 112 * h + 112] * grad_scale).astype(BF16)
        cp = remote(pin.at[1 - c, p], cin.at[p], cs.at[8 + p], cr.at[8 + p], sib)
        cp.start()
        copies.append(cp)

    sum_out = sum_in = None
    for k, step in enumerate(FAR_FIRST + (0,)):
        p = lax.rem(y + step, NY)
        remote(pout.at[c, p], cout.at[p], cs.at[0], cr.at[p], sib).wait_recv()
        s = pout[c, p].astype(F32) + cout[p].astype(F32)
        if k < NY - 1:
            yout[k] = s.astype(BF16)
            cp = remote(yout.at[k], yrout.at[y], ys.at[8 + k], yr.at[8 + y], device(x, z, p, c))
            cp.start()
            copies.append(cp)
        else:
            sum_out = s
    for k in range(NX):
        p = lax.rem(x + 1 + k, NX)
        remote(pin.at[c, p], cin.at[p], cs.at[0], cr.at[8 + p], sib).wait_recv()
        s = pin[c, p].astype(F32) + cin[p].astype(F32)
        if k < NX - 1:
            xin[k] = s.astype(BF16)
            cp = remote(xin.at[k], xrin.at[x], xs.at[k], xr.at[x], device(p, z, y, c))
            cp.start()
            copies.append(cp)
        else:
            sum_in = s

    for k in range(2):
        up = device(x, lax.rem(z + 4 + 8 * k, NZ), y, c)
        pl.semaphore_signal(relay.at[k], inc=1, device_id=up, device_id_type=MESH)

    row, col = lanes((128, 112), 0), lanes((128, 112))
    from_row = 14 * (2 * ((row >> 4) & 3) + ((row >> 3) & 1)) + 7 * (row >> 6) + (row & 7)
    e_in = jnp.where(((row & 7) < 7) & (col == from_row), 1.0, 0.0).astype(BF16)
    row, col = lanes((16, 16), 0), lanes((16, 16))
    turn = (row & 7) + group
    e_out = jnp.where(((row & 7) < 7) & (col == 4 * (row >> 3) + (turn >> 1) + 8 * (turn & 1)), 1.0, 0.0).astype(BF16)
    for p in xpeers:
        remote(xin.at[0], xrin.at[p], xs.at[0], xr.at[p], sib).wait_recv()
        sum_in = sum_in + xrin[p].astype(F32)
    y_in = jnp.dot(e_in, sum_in.astype(BF16), preferred_element_type=F32)
    for p in range(NY):
        ybuf[p] = y_in[16 * p : 16 * p + 16].astype(BF16)
    for k in range(2):
        pl.semaphore_wait(relay.at[k], 1)
    for k, p in enumerate(ypeers):
        cp = remote(ybuf.at[p], yrbuf.at[y], ys.at[k], yr.at[y], device(x, z, p, c))
        cp.start()
        copies.append(cp)

    for p in ypeers:
        remote(yout.at[0], yrout.at[p], ys.at[0], yr.at[8 + p], sib).wait_recv()
        sum_out = sum_out + yrout[p].astype(F32)
    for p in range(NX):
        xout[p] = sum_out[8 * p : 8 * p + 8]
    for k, p in enumerate(xpeers):
        cp = remote(xout.at[p], xrout.at[x], xs.at[4 + k], xr.at[4 + x], device(p, z, y, c))
        cp.start()
        copies.append(cp)
    sum_out = xout[x]
    for p in xpeers:
        remote(xout.at[0], xrout.at[p], xs.at[0], xr.at[4 + p], sib).wait_recv()
        sum_out = sum_out + xrout[p]
    left, right = sum_out[:, :512], pltpu.roll(sum_out[:, 384:], 448, 1)
    halves = jnp.concatenate([left, right], axis=0).astype(BF16)
    y_out = jnp.dot(e_out, halves, preferred_element_type=F32)
    before = pltpu.roll(y_out, 1, 0)
    lane, jrow = lanes((16, 512)), lanes((16, 512), 0) & 7
    flat_out = jnp.zeros((16, 512), F32)
    for k in range(8):
        old = lane < 56 * k + 120
        here, past = pltpu.roll(y_out, (120 + 56 * k) % 512, 1), pltpu.roll(before, (184 + 56 * k) % 512, 1)
        flat_out = jnp.where(jrow == k, jnp.where(old, past, here), flat_out)

    total = ybuf[y].astype(F32)
    for p in ypeers:
        remote(ybuf.at[0], yrbuf.at[p], ys.at[0], yr.at[p], sib).wait_recv()
        total = total + yrbuf[p].astype(F32)

    before = pltpu.roll(total, 1, 0)
    lane, jrow = lanes((16, 640)), lanes((16, 640), 0) & 7
    flat_in = jnp.zeros((16, 640), F32)
    for k in range(8):
        here, past = pltpu.roll(total, 72 * k, 1), pltpu.roll(before, 64 + 72 * k, 1)
        flat_in = jnp.where(jrow == k, jnp.where(lane < 72 * k, past, here), flat_in)
    seam = jnp.where(lanes((16, 128)) < 120, flat_in[:, 384:512], flat_out[:, :128])
    flat = jnp.concatenate([flat_in[:, :384], seam, flat_out[:, 128:], jnp.zeros((16, 128), F32)], axis=1)
    for t in range(8):
        msg[:, t, :] = flat[:, 128 * t : 128 * t + 128].astype(BF16)
    own = 8 * lax.rem(z, 2) + lax.rem(me, 8)

    def target(i):
        n = lax.rem(i, 8)
        return device(x, 8 * c + 2 * quad + lax.div(i, 8), 4 * group + lax.div(n, 2), lax.rem(n, 2))

    for k in range(1, 16):
        i = lax.rem(own + k, 16)
        cp = remote(msg.at[i], rbuf.at[z], fs.at[k], fr.at[z], target(i))
        cp.start()
        copies.append(cp)
    mine = remote(msg.at[own], rbuf.at[z], fs.at[0], fr.at[z], target(own))
    kept = pltpu.make_async_copy(msg.at[own], rbuf.at[z], ls.at[2])

    @pl.when(diagonal)
    def _():
        kept.start()
        kept.wait()

    @pl.when(jnp.logical_not(diagonal))
    def _():
        mine.start()

    hid_load.wait()
    hid = hid_ref[...].astype(F32)
    out = sum(lax.dot_general(a[:, 256 * t : 256 * t + 256], w_ref[2 + t], NT, preferred_element_type=F32) for t in range(2))
    mixed_ref[...] = (hid + out).astype(BF16)
    gn = sum(lax.dot_general(gpa[:, 256 * t : 256 * t + 256], w_ref[t], NT, preferred_element_type=F32) for t in range(2))
    gn = gn + lax.dot_general(gpa[:, 512:], w_ref[2, :, :128], NT, preferred_element_type=F32)
    irms = irms_ref[:, :1]
    normed = hid * irms
    mean = jnp.mean(gn * normed, axis=1, keepdims=True)
    gh_ref[...] = ((gn - normed * mean) * irms + gm.astype(F32)).astype(BF16)

    @pl.when(jnp.logical_not(diagonal))
    def _():
        mine.wait_send()
        remote(msg.at[0], rbuf.at[z], fs.at[0], fr.at[z], sib).wait_recv()

    for k in range(1, 16):
        s = lax.rem(z + k, 16)
        remote(msg.at[0], rbuf.at[s], fs.at[0], fr.at[s], sib).wait_recv()
    total = jnp.sum(rbuf[...].astype(F32), axis=0)
    for t in range(8):
        gout_ref[:, 128 * t : 128 * t + 128] = total[t : t + 1]
    for cp in copies:
        cp.wait_send()


def write_kernel(mixed_ref, gh_ref, grads_ref, mixed_out, gh_out, in_out, out_out, part_in, part_out, sem):
    pairs = ((mixed_ref, mixed_out), (gh_ref, gh_out), (part_in, in_out), (part_out, out_out))
    copies = [pltpu.make_async_copy(src, dst, sem.at[k]) for k, (src, dst) in enumerate(pairs)]
    for cp in copies[:2]:
        cp.start()
    flat = grads_ref[...]
    part_in[...] = flat[:, :504]
    part_out[...] = pltpu.roll(flat, 520, 1)[:, :392]
    for cp in copies[2:]:
        cp.start()
    for cp in copies:
        cp.wait()


def body(hidden_in, doc_ids, grad_mixed, in_codes, in_scales, out_codes, out_scales):
    vm = pl.BlockSpec(memory_space=VMEM)
    hbm = pl.BlockSpec(memory_space=pltpu.HBM)
    dma = pltpu.SemaphoreType.DMA
    sds = jax.ShapeDtypeStruct
    tokens = sds((TOK, D), BF16)
    square = sds((TOK, 128), F32)
    held = [pltpu.with_memory_space_constraint(v, pltpu.HBM) for v in (in_codes, out_codes.T, in_scales.T, out_scales, hidden_in, doc_ids)]
    grad_mixed = pltpu.with_memory_space_constraint(grad_mixed, pltpu.HBM)
    w, *rest = pl.pallas_call(
        gather_kernel,
        out_shape=(sds((4, 8, 2, 56, 256), BF16), tokens, sds((D, TOK), BF16), square, square, square, square),
        in_specs=[hbm] * 6,
        out_specs=(vm,) * 7,
        scratch_shapes=[
            VMEM((56, 576), BF16), VMEM((56, 448), BF16), VMEM((9, 28), F32), VMEM((7, 28), F32),
            VMEM((TOK, D), BF16), VMEM((1, 128), jnp.int32), VMEM((56, 128), F32),
            dma((6,)), dma, dma, dma((8,)), dma, dma((4, 8)), dma, dma,
        ],
        compiler_params=pltpu.CompilerParams(collective_id=0, has_side_effects=True, vmem_limit_bytes=16 << 20),
        name="gather",
    )(*held)
    mixed, grad_hidden, grads = pl.pallas_call(
        main_kernel,
        out_shape=(tokens, tokens, sds((1, 1024), F32)),
        in_specs=[vm, hbm, hbm] + [vm] * 6,
        out_specs=(vm, vm, vm),
        scratch_shapes=[
            VMEM((TOK, D), BF16), VMEM((TOK, D), BF16),
            VMEM((2, 4, 112, 640), BF16), VMEM((2, 8, 32, 896), BF16),
            VMEM((4, 112, 640), BF16), VMEM((8, 32, 896), BF16),
            VMEM((3, 112, 640), BF16), VMEM((4, 8, 896), F32),
            VMEM((4, 112, 640), BF16), VMEM((4, 8, 896), F32),
            VMEM((7, 32, 896), BF16), VMEM((8, 32, 896), BF16),
            VMEM((8, 16, 640), BF16), VMEM((8, 16, 640), BF16),
            VMEM((16, 8, 128), BF16), VMEM((16, 8, 128), BF16),
            dma((12,)), dma((12,)), dma((8,)), dma((8,)), dma((15,)), dma((16,)), dma((16,)), dma((16,)), dma((3,)), pltpu.SemaphoreType.REGULAR((2,)),
        ],
        compiler_params=pltpu.CompilerParams(collective_id=1, has_side_effects=True, vmem_limit_bytes=32 << 20),
        name="sublayer",
    )(w.reshape(4, D, 256), held[4], grad_mixed, *rest)
    mixed, grad_hidden, grad_in, grad_out = pl.pallas_call(
        write_kernel,
        out_shape=(pltpu.HBM((TOK, D), BF16), pltpu.HBM((TOK, D), BF16), pltpu.HBM((1, 504), F32), pltpu.HBM((1, 392), F32)),
        in_specs=[vm] * 3,
        out_specs=(hbm,) * 4,
        scratch_shapes=[VMEM((1, 504), F32), VMEM((1, 392), F32), dma((4,))],
        name="write",
    )(*(pltpu.with_memory_space_constraint(v, VMEM) for v in (mixed, grad_hidden, grads)))
    return mixed, grad_hidden, grad_in.reshape(504), grad_out.reshape(392)


def solution(mesh):
    rows = P(("outer", "inner"), None)
    return jax.shard_map(
        body,
        mesh=mesh,
        in_specs=(rows, rows, rows, P("inner", None), P(), P(None, "inner"), P()),
        out_specs=(rows, rows, P(("outer", "inner")), P(("outer", "inner"))),
        check_vma=False,
    )
```
